32 devices in a mesh: groups: 2 (over y), gx: 4 (over x, core), gy: 4 (over z).
Axes of the slice: x: 2, y: 2, z: 4, core: 2. Of those that a mesh axis runs over, the one named last changes fastest.
Arguments:
- theta: float32 [32, 128, 512], P('groups', 'gx', 'gy'), parts along dimension 0, may hold values from -6 to 6
- terrain: float32 [256, 512], P(('groups', 'gx'), 'gy'), parts along dimension 0, may hold values from 0.5 to 2
- head: float32 [16, 256, 1024], P('groups', 'gy', 'gx'), parts along dimension 0, may hold values from -5 to -0.1
- soil: int32 [512, 1024], P(('groups', 'gy'), 'gx'), parts along dimension 0, may hold values from 0 to 7
- pair_map: int32 [8, 2], replicated, may hold values from 0 to 3
- tiles: float32 [8, 2, 128, 128], replicated, may hold values from -0.375 to 0.375
- vg_alpha: float32 [8], replicated, may hold values from 0.5 to 4
- vg_n: float32 [8], replicated, may hold values from 1.3 to 3
- ksat: float32 [8], replicated, may hold values from 0.05 to 1
Outputs:
- theta_next: float32 [32, 128, 512], P('groups', 'gx', 'gy'), parts along dimension 0
- head_next: float32 [16, 256, 1024], P('groups', 'gy', 'gx'), parts along dimension 0
The draws below stay inside these ranges and needn't reach their ends.
There are 2 independent parts, one for each index of `groups`. The reference program is written for one: setup_inputs(seed, part) draws one part's arguments, and reference() takes and returns one part's arrays. A program takes and returns all parts, laid end to end along the dimension named above; an argument that names none is the same for every part. Nothing has to cross between parts.
All inputs are finite; a program needn't handle non-finite values.
Results may differ from the reference program's by a relative error of at most 0.00014.
Values sent between devices are 32-bit elements; how exact they have to be, the bound alone decides.
A program may use at most 64 MiB of HBM per device.

```python
import math
import jax
import jax.numpy as jnp
from jax import lax

LEV = 16
LEVS = 8
ABLK = 128
ITERS = 3
NSWEEP = 2
NSOIL = 8
AX = 128
AY = 512
SX = 256
SY = 1024
NBA = 4
NBS = 8


def touch_ends(values, rng, low, high):
    index_at = [jax.random.randint(jax.random.fold_in(rng, axis), (), 0, length) for axis, length in enumerate(values.shape)]
    main_axis = values.shape.index(max(values.shape))
    neighbour = index_at[:main_axis] + [(index_at[main_axis] + 1) % values.shape[main_axis]] + index_at[main_axis + 1:]
    return values.at[tuple(index_at)].set(low).at[tuple(neighbour)].set(high)


def block_scale(rng, extent, cuts, least, top_value):
    level, own = 1.0, jax.random.fold_in(rng, 6)
    for dim, blocks in cuts:
        steps = jnp.exp(jax.random.uniform(jax.random.fold_in(own, dim), (blocks,), jnp.float32, least / len(cuts), top_value / len(cuts)))
        level = level * jnp.repeat(steps, extent[dim] // blocks).reshape([-1 if axis == dim else 1 for axis in range(len(extent))])
    return level


def noise(key, dims, scale, limit, cuts=(), kind=jnp.bfloat16):
    array = jax.random.normal(key, dims, jnp.float32) * scale
    if len(cuts) > 0:
        array = block_scale(key, dims, cuts, -0.22, 0.18) * array
    return jnp.clip(array, min=-limit, max=limit).astype(kind)


def setup_inputs(seed: int = 0, part: int = 0) -> dict:
    streams_of = jax.random.split(jax.random.key(seed), 10)
    part_splits = jax.random.split(jax.random.fold_in(streams_of[9], part), 10)
    theta = noise(part_splits[0], (LEV, AX, AY), 1.0, 6.0, ((1, 4), (2, 4)), jnp.float32)
    terrain = jnp.clip(0.5 + 1.5 * jax.random.uniform(part_splits[1], (AX, AY), jnp.float32) ** block_scale(part_splits[1], (AX, AY), ((0, 4), (1, 4)), -0.2, 0.2), 0.5, 2.0)
    head = jnp.clip(-5.0 + 4.9 * jax.random.uniform(part_splits[2], (LEVS, SX, SY), jnp.float32) ** block_scale(part_splits[2], (LEVS, SX, SY), ((1, 4), (2, 4)), -0.2, 0.2), -5.0, -0.1)
    soil = touch_ends(jax.random.randint(part_splits[3], (SX, SY), 0, NSOIL), jax.random.fold_in(part_splits[3], 1), 0, NSOIL - 1).astype(jnp.int32)
    pair_map = touch_ends(jax.random.randint(streams_of[4], (NBS, 2), 0, NBA), jax.random.fold_in(streams_of[4], 1), 0, NBA - 1).astype(jnp.int32)
    tiles = noise(streams_of[5], (NBS, 2, ABLK, ABLK), (2 * ABLK) ** -0.5, 0.375, (), jnp.float32)
    vg_alpha = jnp.clip(jnp.exp(jax.random.uniform(streams_of[6], (NSOIL,), jnp.float32, math.log(0.5), math.log(4.0))), 0.5, 4.0)
    vg_n = jnp.clip(jax.random.uniform(streams_of[7], (NSOIL,), jnp.float32, 1.3, 3.0), 1.3, 3.0)
    ksat = jnp.clip(jnp.exp(jax.random.uniform(streams_of[8], (NSOIL,), jnp.float32, math.log(0.05), math.log(1.0))), 0.05, 1.0)
    return dict(theta=theta, terrain=terrain, head=head, soil=soil, pair_map=pair_map, tiles=tiles, vg_alpha=vg_alpha, vg_n=vg_n, ksat=ksat)


diffuse = 0.08
vertical_mix = 0.1
time_step = 4.0
infiltrate = 0.5
evaporate = 1.0
storage = 0.1

def regrid_down(rows, pair_map, tiles):
    width = tiles.shape[2]
    nblock = rows.shape[1] // width
    blocks = rows.reshape(rows.shape[0], nblock, width)
    chosen = jnp.take(blocks, pair_map, axis=1)
    result = jnp.einsum('rsqa,sqab->rsb', chosen, tiles, precision=lax.Precision.HIGHEST)
    return jnp.repeat(result.reshape(rows.shape[0], -1), 2, axis=0)

def regrid_up(field, pair_map, tiles, nblock):
    width = tiles.shape[2]
    paired = field.reshape(field.shape[0] // 2, 2, field.shape[1])
    halves = 0.5 * (paired[:, 0] + paired[:, 1])
    blocks = halves.reshape(halves.shape[0], tiles.shape[0], width)
    contrib = jnp.einsum('rsb,sqab->rsqa', blocks, tiles, precision=lax.Precision.HIGHEST)
    onehot = (pair_map[:, :, None] == jnp.arange(nblock, dtype=jnp.int32)[None, None, :]).astype(jnp.float32)
    result = jnp.einsum('rsqa,sqn->rna', contrib, onehot, precision=lax.Precision.HIGHEST)
    return result.reshape(halves.shape[0], nblock * width)

def soil_state(head, alpha, expo, kmax):
    expo_m = 1.0 - 1.0 / expo
    sat = (1.0 + (alpha * jnp.abs(head)) ** expo) ** (-expo_m)
    inner = 1.0 - (1.0 - sat ** (1.0 / expo_m)) ** expo_m
    return (sat, kmax * jnp.sqrt(sat) * inner * inner)

def face_coeffs(padded):
    centre = padded[1:-1, 1:-1, 1:-1]
    return (jnp.sqrt(centre * padded[2:, 1:-1, 1:-1]), jnp.sqrt(centre * padded[:-2, 1:-1, 1:-1]), jnp.sqrt(centre * padded[1:-1, 2:, 1:-1]), jnp.sqrt(centre * padded[1:-1, :-2, 1:-1]), jnp.sqrt(centre * padded[1:-1, 1:-1, 2:]), jnp.sqrt(centre * padded[1:-1, 1:-1, :-2]))

def apply_faces(faces, padded):
    centre = padded[1:-1, 1:-1, 1:-1]
    total = faces[0] * (centre - padded[2:, 1:-1, 1:-1]) + faces[1] * (centre - padded[:-2, 1:-1, 1:-1])
    total = total + faces[2] * (centre - padded[1:-1, 2:, 1:-1]) + faces[3] * (centre - padded[1:-1, :-2, 1:-1])
    total = total + faces[4] * (centre - padded[1:-1, 1:-1, 2:]) + faces[5] * (centre - padded[1:-1, 1:-1, :-2])
    return total

def advance(padded, metric):
    centre = padded[:, 1:-1, 1:-1]
    flat = padded[:, 2:, 1:-1] + padded[:, :-2, 1:-1] + padded[:, 1:-1, 2:] + padded[:, 1:-1, :-2] - 4.0 * centre
    column = jnp.pad(centre, ((1, 1), (0, 0), (0, 0)))
    vert = column[2:] + column[:-2] - 2.0 * centre
    return centre + diffuse * metric * flat + vertical_mix * vert

def reference(theta, terrain, head, soil, pair_map, tiles, vg_alpha, vg_n, ksat):
    infil = regrid_down(theta[0], pair_map, tiles)
    alpha = jnp.take(vg_alpha, soil, axis=0)[None]
    expo = jnp.take(vg_n, soil, axis=0)[None]
    kmax = jnp.take(ksat, soil, axis=0)[None]
    sat, cond = soil_state(head, alpha, expo, kmax)
    capacity = (storage + sat) / time_step
    faces = face_coeffs(jnp.pad(cond, 1))
    rhs = faces[0] - faces[1] - apply_faces(faces, jnp.pad(head, 1))
    rhs = rhs.at[0].add(infiltrate * infil)
    delta = jnp.zeros_like(head)
    resid = rhs
    direction = rhs
    norm_now = jnp.sum(resid * resid)
    for step in range(ITERS):
        image = capacity * direction + apply_faces(faces, jnp.pad(direction, 1))
        alpha_step = norm_now / jnp.sum(direction * image)
        delta = delta + alpha_step * direction
        resid = resid - alpha_step * image
        norm_next = jnp.sum(resid * resid)
        direction = resid + norm_next / norm_now * direction
        norm_now = norm_next
    head_next = head + delta
    moist, unused = soil_state(head_next[0], alpha[0], expo[0], kmax[0])
    back = regrid_up(moist, pair_map, tiles, theta.shape[2] // tiles.shape[2])
    swept = theta
    for sweep in range(NSWEEP):
        swept = advance(jnp.pad(swept, ((0, 0), (1, 1), (1, 1))), terrain)
    theta_next = swept.at[0].add(evaporate * back)
    return (theta_next, head_next)
```

```python
import functools

import jax
import jax.numpy as jnp
from jax import lax
from jax.experimental import pallas as pl
from jax.experimental.pallas import tpu as pltpu
from jax.sharding import PartitionSpec as P

diffuse = 0.08
vertical_mix = 0.1
time_step = 4.0
infiltrate = 0.5
evaporate = 1.0
storage = 0.1

LANES = 128
SUB = 8
MESH = pl.DeviceIdType.MESH
HIGH = lax.Precision.HIGHEST
F32 = jnp.float32


def dot(a, b):
    return jnp.dot(a, b, precision=HIGH, preferred_element_type=F32)


def dot_nt(a, b):
    return lax.dot_general(
        a, b, (((1,), (1,)), ((), ())), precision=HIGH, preferred_element_type=F32
    )


def each(count, body):
    if count <= 16:
        for index in range(count):
            body(index)
    else:

        @pl.loop(0, count)
        def _(index):
            body(index)


def turn(value, amount, axis):
    size = value.shape[axis]
    amount = amount % size
    return value if amount == 0 else pltpu.roll(value, amount, axis)


def retention(head, alpha, expo):
    expo_m = 1.0 - 1.0 / expo
    power = expo * jnp.log(alpha * jnp.abs(head))
    log_u = jnp.log(1.0 + jnp.exp(power))
    return power, log_u, expo_m, jnp.exp(-0.25 * expo_m * log_u)


def pick(kind, table_ref):
    value = jnp.full(kind.shape, table_ref[0], F32)
    for index in range(1, table_ref.shape[0]):
        value = jnp.where(kind == float(index), table_ref[index], value)
    return value


def kernel(
    ngx,
    ngy,
    theta_hbm,
    terrain_hbm,
    head_hbm,
    soil_hbm,
    tiles_hbm,
    pair_ref,
    alpha_ref,
    expo_ref,
    ksat_ref,
    theta_out,
    head_out,
    th,
    sw,
    done,
    tr,
    hd,
    soil,
    soilf,
    tl,
    rowh,
    rows_soil,
    pack,
    colr,
    corner,
    gath,
    trs,
    trr,
    tcs,
    tcr,
    root,
    cap,
    diag,
    vec0,
    vec1,
    vec2,
    wvec,
    mom,
    momr,
    bsend,
    brecv,
    local_sem,
    out_sem,
    near_send,
    near_recv,
    g_send,
    g_recv,
    t_send,
    t_recv,
    m_send,
    m_recv,
    b_send,
    b_recv,
):
    x = lax.axis_index("gx")
    y = lax.axis_index("gy")
    levs, height, width = head_hbm.shape
    lev, th_rows, _ = theta_hbm.shape
    tile_count = width // LANES
    nblock = gath.shape[0]
    ratio = height // 2 // th_rows
    group = ngx * ngy
    me = x * ngy + y
    ext_h, ext_w = height + SUB, width + LANES
    low, high_x = x > 0, x < ngx - 1
    left, right_y = y > 0, y < ngy - 1

    loads = []

    def load(src, dst):
        copy = pltpu.make_async_copy(src, dst, local_sem.at[len(loads)])
        copy.start()
        loads.append(copy)
        return copy

    c_theta = load(theta_hbm, th)
    c_head = load(head_hbm, hd.at[:, 0:height, 0:width])
    c_soil = load(soil_hbm, soil)
    c_terrain = load(terrain_hbm, tr)
    first = x * tile_count
    total_tiles = tiles_hbm.shape[0]
    tile_at = [
        jnp.minimum(jnp.maximum(first + i - 1, 0), total_tiles - 1)
        for i in range(tile_count + 2)
    ]
    c_tiles = [load(tiles_hbm.at[tile_at[i]], tl.at[i]) for i in range(tile_count + 2)]

    rowh[...] = jnp.zeros(rowh.shape, F32)
    rows_soil[...] = jnp.zeros(rows_soil.shape, jnp.int32)
    colr[...] = jnp.zeros(colr.shape, F32)
    corner[...] = jnp.zeros(corner.shape, F32)
    gath[...] = jnp.zeros(gath.shape, F32)
    trr[...] = jnp.zeros(trr.shape, F32)
    tcr[...] = jnp.zeros(tcr.shape, F32)

    barrier = pltpu.get_barrier_semaphore()

    def greet(index):
        @pl.when(index != me)
        def _():
            pl.semaphore_signal(
                barrier,
                inc=1,
                device_id={"gx": index // ngy, "gy": index % ngy},
                device_id_type=MESH,
            )

    each(group, greet)

    lane = lax.broadcasted_iota(jnp.int32, (1, LANES), 1)

    def pack_theta(sweep, source):
        trs[sweep, 0] = source[:, 0, :]
        trs[sweep, 1] = source[:, th_rows - 1, :]
        first_col = jnp.zeros((th_rows, LANES), F32)
        last_col = jnp.zeros((th_rows, LANES), F32)
        for k in range(lev):
            first_col = jnp.where(lane == k, turn(source[k], k, 1), first_col)
            last_col = jnp.where(lane == k, turn(source[k], k + 1, 1), last_col)
        tcs[sweep, 0] = first_col
        tcs[sweep, 1] = last_col

    c_theta.wait()
    pack_theta(0, th)

    c_head.wait()
    c_soil.wait()
    soilf[0:height, 0:width] = soil[...].astype(F32)
    edge_l = jnp.zeros((height, LANES), F32)
    edge_r = jnp.zeros((height, LANES), F32)
    for k in range(levs + 1):
        if k < levs:
            a, b = hd[k, 0:height, 0:LANES], hd[k, 0:height, width - LANES : width]
        else:
            a, b = soilf[0:height, 0:LANES], soilf[0:height, width - LANES : width]
        edge_l = jnp.where(lane // 4 == k, turn(a, 4 * k, 1), edge_l)
        edge_r = jnp.where((LANES - 1 - lane) // 4 == k, turn(b, -4 * k, 1), edge_r)
    pack[0] = edge_l
    pack[1] = edge_r

    pl.semaphore_wait(barrier, group - 1)

    sent = []

    def remote(src, dst, ssem, rsem, to):
        return pltpu.make_async_remote_copy(
            src_ref=src,
            dst_ref=dst,
            send_sem=ssem,
            recv_sem=rsem,
            device_id={"gx": to[0], "gy": to[1]},
            device_id_type=MESH,
        )

    def send(cond, *what):
        @pl.when(cond)
        def _():
            remote(*what).start()

        sent.append((cond, what))

    def arrive(cond, dst, rsem):
        @pl.when(cond)
        def _():
            remote(dst, dst, near_send.at[0], rsem, (x, y)).wait_recv()

    near = []

    def halo(index, cond, src, dst, to, cond_in):
        send(cond, src, dst, near_send.at[index], near_recv.at[index], to)
        near.append((cond_in, dst, near_recv.at[index]))

    halo(0, left, head_hbm.at[:, 0:SUB, :], rowh.at[0], (x, y - 1), right_y)
    halo(1, right_y, head_hbm.at[:, height - SUB :, :], rowh.at[1], (x, y + 1), left)
    halo(2, low, pack.at[0], colr.at[0], (x - 1, y), high_x)
    halo(3, high_x, pack.at[1], colr.at[1], (x + 1, y), low)

    dest = x // ratio
    part = x % ratio
    offset = pl.multiple_of(part * th_rows, th_rows)
    body = ratio * th_rows

    def spread(kind, cond, dest_y, src, dst, slot):
        def one(i):
            me_too = jnp.logical_and(i == x, dest_y == y)

            @pl.when(jnp.logical_and(cond, jnp.logical_not(me_too)))
            def _():
                remote(
                    src, dst, g_send.at[kind, i], g_recv.at[kind, slot], (i, dest_y)
                ).start()

        each(ngx, one)

        @pl.when(jnp.logical_and(cond, dest_y == y))
        def _():
            dst[...] = src[...]

        def finish(i):
            me_too = jnp.logical_and(i == x, dest_y == y)

            @pl.when(jnp.logical_and(cond, jnp.logical_not(me_too)))
            def _():
                remote(
                    src, dst, g_send.at[kind, i], g_recv.at[kind, slot], (i, dest_y)
                ).wait_send()

        return lambda: each(ngx, finish)

    slot = y * ratio + part
    at_first, at_last = part == 0, part == ratio - 1
    finish_spread = [
        spread(0, x >= 0, dest, th.at[0], gath.at[y, pl.ds(offset, th_rows)], slot),
        spread(
            1,
            jnp.logical_and(at_first, dest > 0),
            dest - 1,
            th.at[0, 0:SUB],
            gath.at[y, body : body + SUB],
            y,
        ),
        spread(
            2,
            jnp.logical_and(at_last, dest < ngy - 1),
            dest + 1,
            th.at[0, th_rows - SUB : th_rows],
            gath.at[y, body + SUB : body + 2 * SUB],
            y,
        ),
    ]

    halo(4, left, soil_hbm.at[0:SUB, :], rows_soil.at[0], (x, y - 1), right_y)
    halo(5, right_y, soil_hbm.at[height - SUB :, :], rows_soil.at[1], (x, y + 1), left)
    both = jnp.logical_and
    halo(6, both(low, left), pack.at[0, 0:SUB], corner.at[0], (x - 1, y - 1), both(high_x, right_y))
    halo(7, both(low, right_y), pack.at[0, height - SUB :], corner.at[1], (x - 1, y + 1), both(high_x, left))
    halo(8, both(high_x, left), pack.at[1, 0:SUB], corner.at[2], (x + 1, y - 1), both(low, right_y))
    halo(9, both(high_x, right_y), pack.at[1, height - SUB :], corner.at[3], (x + 1, y + 1), both(low, left))

    theta_in = []

    def theta_halo(sweep):
        got = []
        plan = (
            (low, trs, trr, 0, (x - 1, y), high_x),
            (high_x, trs, trr, 1, (x + 1, y), low),
            (left, tcs, tcr, 0, (x, y - 1), right_y),
            (right_y, tcs, tcr, 1, (x, y + 1), left),
        )
        for index, (cond, src, dst, side, to, cond_in) in enumerate(plan):
            send(
                cond,
                src.at[sweep, side],
                dst.at[sweep, side],
                t_send.at[sweep, index],
                t_recv.at[sweep, index],
                to,
            )
            got.append((cond_in, dst.at[sweep, side], t_recv.at[sweep, index]))
        theta_in.append(got)

    theta_halo(0)

    def state(k, rows, cols, alpha, expo, kmax, mask):
        power, log_u, expo_m, quarter = retention(hd[k, rows, cols], alpha, expo)
        sat = (quarter * quarter) * (quarter * quarter)
        cap[k, rows, cols] = (storage + sat) * (1.0 / time_step)
        value = jnp.sqrt(kmax) * quarter * (1.0 - jnp.exp(expo_m * (power - log_u)))
        root[k, rows, cols] = value if mask is None else jnp.where(mask, value, 0.0)

    def state_block(rows, cols, mask):
        kind = soilf[rows, cols]
        alpha, expo, kmax = (
            pick(kind, alpha_ref),
            pick(kind, expo_ref),
            pick(kind, ksat_ref),
        )
        for k in range(levs):
            state(k, rows, cols, alpha, expo, kmax, mask)

    for row in range(0, height, 32):
        state_block(slice(row, row + 32), slice(0, width), None)

    def sweep_once(sweep, source, store):
        for cond, dst, sem in theta_in[sweep]:
            arrive(cond, dst, sem)
        row_at = lax.broadcasted_iota(jnp.int32, (th_rows, LANES), 0)
        metric = diffuse * tr[...]
        from_right, from_left = tcr[sweep, 0], tcr[sweep, 1]
        for k in range(lev):
            centre = source[k]
            down = jnp.where(
                row_at == th_rows - 1, trr[sweep, 0, k : k + 1, :], turn(centre, -1, 0)
            )
            up = jnp.where(row_at == 0, trr[sweep, 1, k : k + 1, :], turn(centre, 1, 0))
            east = jnp.where(
                lane == LANES - 1, turn(from_right, LANES - 1 - k, 1), turn(centre, -1, 1)
            )
            west = jnp.where(lane == 0, turn(from_left, -k, 1), turn(centre, 1, 1))
            flat = down + up + east + west - 4.0 * centre
            vert = -2.0 * centre
            if k > 0:
                vert = vert + source[k - 1]
            if k < lev - 1:
                vert = vert + source[k + 1]
            store(k, centre + metric * flat + vertical_mix * vert)

    def store_first(k, value):
        sw[k] = value

    c_terrain.wait()
    sweep_once(0, th, store_first)
    pack_theta(1, sw)
    theta_halo(1)

    for cond, dst, sem in near:
        arrive(cond, dst, sem)
    upper = lax.broadcasted_iota(jnp.int32, (SUB, 1), 0) < 4
    first_half = lane < LANES // 2
    for k in range(levs):
        hd[k, height:ext_h, 0:width] = jnp.where(upper, rowh[0, k], rowh[1, k])
    soilf[height:ext_h, 0:width] = jnp.where(upper, rows_soil[0], rows_soil[1]).astype(F32)
    right_side, left_side = colr[0], colr[1]
    right_corner = jnp.where(upper, corner[0], corner[1])
    left_corner = jnp.where(upper, corner[2], corner[3])
    for k in range(levs + 1):
        side = jnp.where(first_half, turn(right_side, -4 * k, 1), turn(left_side, 4 * k, 1))
        tip = jnp.where(first_half, turn(right_corner, -4 * k, 1), turn(left_corner, 4 * k, 1))
        if k < levs:
            hd[k, 0:height, width:ext_w] = side
            hd[k, height:ext_h, width:ext_w] = tip
        else:
            soilf[0:height, width:ext_w] = side
            soilf[height:ext_h, width:ext_w] = tip

    col_ok = jnp.logical_or(
        jnp.logical_and(lane < 4, high_x), jnp.logical_and(lane >= LANES - 4, low)
    )
    row_ok = jnp.logical_or(
        jnp.logical_and(upper, right_y), jnp.logical_and(jnp.logical_not(upper), left)
    )
    state_block(
        slice(0, height), slice(width, ext_w), jnp.broadcast_to(col_ok, (height, LANES))
    )
    state_block(
        slice(height, ext_h), slice(0, width), jnp.broadcast_to(row_ok, (SUB, width))
    )
    state_block(
        slice(height, ext_h), slice(width, ext_w), jnp.logical_and(row_ok, col_ok)
    )

    def arrive_blocks(kind, cond, from_x, dst_of, slot_of):
        def one(b):
            mine = jnp.logical_and(from_x == x, b == y)

            @pl.when(jnp.logical_and(cond, jnp.logical_not(mine)))
            def _():
                dst = dst_of(b)
                remote(dst, dst, near_send.at[0], g_recv.at[kind, slot_of(b)], (x, y)).wait_recv()

        each(nblock, one)

    for r in range(ratio):
        arrive_blocks(
            0,
            x >= 0,
            y * ratio + r,
            lambda b, r=r: gath.at[b, r * th_rows : (r + 1) * th_rows],
            lambda b, r=r: b * ratio + r,
        )
    arrive_blocks(
        1, right_y, (y + 1) * ratio, lambda b: gath.at[b, body : body + SUB], lambda b: b
    )
    arrive_blocks(
        2,
        left,
        y * ratio - 1,
        lambda b: gath.at[b, body + SUB : body + 2 * SUB],
        lambda b: b,
    )
    for copy in c_tiles:
        copy.wait()
    grow_to = lax.broadcasted_iota(jnp.int32, (ext_h, body + 2 * SUB), 0)
    grow_from = lax.broadcasted_iota(jnp.int32, (ext_h, body + 2 * SUB), 1)
    source_row = jnp.where(
        grow_to < height + 4, grow_to // 2, body + 2 * SUB - 2 + (grow_to - height - 4) // 2
    )
    grow = jnp.where(grow_from == source_row, infiltrate, 0.0).astype(F32)

    def down(i):
        total = None
        for q in range(2):
            term = dot(gath[pair_ref[tile_at[i], q]], tl[i, q])
            total = term if total is None else total + term
        return total

    infil = [dot(grow, down(i + 1)) for i in range(tile_count)]
    ends = jnp.where(first_half, down(tile_count + 1), down(0))
    infil.append(dot(grow, ends))

    def across(value):
        return (turn(value, 1, 1) + turn(value, -1, 1)) + (
            turn(value, 1, 0) + turn(value, -1, 0)
        )

    def around(ref, k):
        total = across(ref[k])
        if k > 0:
            total = total + ref[k - 1]
        if k < levs - 1:
            total = total + ref[k + 1]
        return total

    for k in range(levs):
        wvec[0, k] = root[k] * hd[k]
    for k in range(levs):
        centre = root[k]
        span = around(root, k)
        flow = around(wvec.at[0], k) - span * hd[k]
        if k > 0:
            flow = flow - root[k - 1]
        if k < levs - 1:
            flow = flow + root[k + 1]
        rhs = centre * flow
        if k == 0:
            rhs = rhs + jnp.concatenate(infil, axis=1)
        diag[k] = cap[k] + centre * span
        vec0[k] = rhs
        wvec[1, k] = centre * rhs

    def fold(value):
        part = None
        for c in range(0, width, LANES):
            for r in range(0, height, SUB):
                piece = value[r : r + SUB, c : c + LANES]
                part = piece if part is None else part + piece
        return part

    def plus(total, value):
        return value if total is None else total + value

    sums = [None] * 6
    for k in range(levs):
        here = vec0[k]
        image = diag[k] * here - root[k] * around(wvec.at[1], k)
        vec1[k] = image
        wvec[0, k] = root[k] * image
        sums[0] = plus(sums[0], fold(here * here))
        sums[1] = plus(sums[1], fold(here * image))
        sums[2] = plus(sums[2], fold(image * image))
    for k in range(levs):
        here = vec1[k]
        image = diag[k] * here - root[k] * around(wvec.at[0], k)
        vec2[k] = image
        wvec[1, k] = root[k] * image
        sums[3] = plus(sums[3], fold(here * image))
        sums[4] = plus(sums[4], fold(image * image))
    for k in range(levs):
        here = vec2[k]
        image = diag[k] * here - root[k] * around(wvec.at[1], k)
        sums[5] = plus(sums[5], fold(here * image))

    row8 = lax.broadcasted_iota(jnp.int32, (SUB, LANES), 0)
    packed = jnp.zeros((SUB, LANES), F32)
    for index, value in enumerate(sums):
        packed = jnp.where(row8 == index, jnp.sum(value, axis=0, keepdims=True), packed)
    mom[...] = packed
    momr[me] = packed

    def tell(index):
        @pl.when(index != me)
        def _():
            remote(
                mom, momr.at[me], m_send.at[index], m_recv.at[me], (index // ngy, index % ngy)
            ).start()

    each(group, tell)

    def store_second(k, value):
        done[k] = value

    sweep_once(1, sw, store_second)
    out_theta = pltpu.make_async_copy(done.at[1:lev], theta_out.at[1:lev], out_sem.at[0])
    out_theta.start()

    def hear(index):
        @pl.when(index != me)
        def _():
            remote(mom, momr.at[index], near_send.at[0], m_recv.at[index], (x, y)).wait_recv()

    each(group, hear)
    moments = jnp.sum(jnp.sum(momr[...], axis=0), axis=1, keepdims=True)
    mu = [moments[i : i + 1, :] for i in range(6)]
    scale = mu[1] / mu[0]
    inverse = mu[0] / mu[1]
    nu = []
    factor = 1.0 / mu[0]
    for i in range(6):
        nu.append(mu[i] * factor)
        factor = factor * inverse
    tiny = 1e-7
    l1, l2 = nu[2] / nu[1], nu[3] / nu[1]
    a11 = jnp.maximum(nu[3] - l1 * nu[2], tiny * nu[3])
    a12 = nu[4] - l1 * nu[3]
    b1 = nu[1] - l1 * nu[0]
    ratio_l = a12 / a11
    a22 = jnp.maximum(nu[5] - l2 * nu[3] - ratio_l * a12, tiny * nu[5])
    b2 = nu[2] - l2 * nu[0] - ratio_l * b1
    c2 = b2 / a22
    c1 = (b1 - a12 * c2) / a11
    c0 = (nu[0] - nu[2] * c1 - nu[3] * c2) / nu[1]
    c0 = c0 * inverse
    c1 = c1 * inverse * inverse
    c2 = c2 * inverse * inverse * inverse

    def advance_head(k):
        own = (k, slice(0, height), slice(0, width))
        value = hd[own] + (c0 * vec0[own] + c1 * vec1[own] + c2 * vec2[own])
        hd[own] = value
        return value

    surface = advance_head(0)
    kind = soilf[0:height, 0:width]
    _, _, _, quarter = retention(surface, pick(kind, alpha_ref), pick(kind, expo_ref))
    moist = (quarter * quarter) * (quarter * quarter)
    pair_row = lax.broadcasted_iota(jnp.int32, (body, height), 0)
    pair_col = lax.broadcasted_iota(jnp.int32, (body, height), 1)
    halver = jnp.where(pair_col // 2 == pair_row, 0.5, 0.0).astype(F32)
    halves = dot(halver, moist)
    contrib = []
    for i in range(tile_count):
        for q in range(2):
            contrib.append(
                (
                    pair_ref[first + i, q],
                    dot_nt(halves[:, i * LANES : (i + 1) * LANES], tl[i + 1, q]),
                )
            )

    for t in range(nblock):
        total = jnp.zeros((body, LANES), F32)
        for where_to, value in contrib:
            total = total + jnp.where(where_to == t, value, 0.0)
        for r in range(ratio):
            piece = total[r * th_rows : (r + 1) * th_rows]
            bsend[t * ratio + r] = piece
            to_x = y * ratio + r
            mine = jnp.logical_and(to_x == x, y == t)

            @pl.when(mine)
            def _():
                brecv[x] = piece

            @pl.when(jnp.logical_not(mine))
            def _():
                remote(
                    bsend.at[t * ratio + r],
                    brecv.at[x],
                    b_send.at[t * ratio + r],
                    b_recv.at[x],
                    (to_x, t),
                ).start()

    for k in range(1, levs):
        advance_head(k)
    out_head = pltpu.make_async_copy(
        hd.at[:, 0:height, 0:width], head_out, out_sem.at[1]
    )
    out_head.start()

    own_y = x // ratio

    def collect(index):
        mine = jnp.logical_and(index == x, own_y == y)

        @pl.when(jnp.logical_not(mine))
        def _():
            remote(
                brecv.at[index], brecv.at[index], near_send.at[0], b_recv.at[index], (x, y)
            ).wait_recv()

    each(ngx, collect)
    done[0] = done[0] + evaporate * jnp.sum(brecv[...], axis=0)
    out_level = pltpu.make_async_copy(done.at[0], theta_out.at[0], out_sem.at[2])
    out_level.start()

    for cond, what in sent:

        @pl.when(cond)
        def _():
            remote(*what).wait_send()

    for finish in finish_spread:
        finish()

    def told(index):
        @pl.when(index != me)
        def _():
            remote(
                mom, momr.at[me], m_send.at[index], m_recv.at[me], (index // ngy, index % ngy)
            ).wait_send()

    each(group, told)
    for t in range(nblock):
        for r in range(ratio):
            to_x = y * ratio + r

            @pl.when(jnp.logical_not(jnp.logical_and(to_x == x, y == t)))
            def _():
                remote(
                    bsend.at[t * ratio + r],
                    brecv.at[x],
                    b_send.at[t * ratio + r],
                    b_recv.at[x],
                    (to_x, t),
                ).wait_send()

    out_theta.wait()
    out_head.wait()
    out_level.wait()


def shards(ngx, ngy, theta, terrain, head, soil, pair_map, tiles, vg_alpha, vg_n, ksat):
    lev, th_rows, _ = theta.shape
    levs, height, width = head.shape
    body = height // 2
    ratio = body // th_rows
    tile_count = width // LANES
    ext = (levs, height + SUB, width + LANES)
    dma = pltpu.SemaphoreType.DMA
    group = ngx * ngy
    anywhere = pl.BlockSpec(memory_space=pl.ANY)
    scalars = pl.BlockSpec(memory_space=pltpu.SMEM)
    vmem = lambda *shape: pltpu.VMEM(shape, F32)
    return pl.pallas_call(
        functools.partial(kernel, ngx, ngy),
        out_shape=(
            jax.ShapeDtypeStruct(theta.shape, F32),
            jax.ShapeDtypeStruct(head.shape, F32),
        ),
        in_specs=[anywhere] * 5 + [scalars] * 4,
        out_specs=(anywhere, anywhere),
        scratch_shapes=[
            vmem(*theta.shape),
            vmem(*theta.shape),
            vmem(*theta.shape),
            vmem(*terrain.shape),
            vmem(*ext),
            pltpu.VMEM((height, width), jnp.int32),
            vmem(*ext[1:]),
            vmem(tile_count + 2, 2, LANES, LANES),
            vmem(2, levs, SUB, width),
            pltpu.VMEM((2, SUB, width), jnp.int32),
            vmem(2, height, LANES),
            vmem(2, height, LANES),
            vmem(4, SUB, LANES),
            vmem(ngy, body + 2 * SUB, LANES),
            vmem(2, 2, lev, LANES),
            vmem(2, 2, lev, LANES),
            vmem(2, 2, th_rows, LANES),
            vmem(2, 2, th_rows, LANES),
            vmem(*ext),
            vmem(*ext),
            vmem(*ext),
            vmem(*ext),
            vmem(*ext),
            vmem(*ext),
            vmem(2, *ext),
            vmem(SUB, LANES),
            vmem(group, SUB, LANES),
            vmem(ngy * ratio, th_rows, LANES),
            vmem(ngx, th_rows, LANES),
            dma((tile_count + 6,)),
            dma((3,)),
            dma((10,)),
            dma((10,)),
            dma((3, ngx)),
            dma((3, ngy * ratio)),
            dma((2, 4)),
            dma((2, 4)),
            dma((group,)),
            dma((group,)),
            dma((ngy * ratio,)),
            dma((ngx,)),
        ],
        compiler_params=pltpu.CompilerParams(
            collective_id=0, has_side_effects=True, vmem_limit_bytes=40 * 1024 * 1024
        ),
        name="coupled_step",
    )(theta, terrain, head, soil, tiles, pair_map, vg_alpha, vg_n, ksat)


def solution(mesh):
    placed = (
        P("groups", "gx", "gy"),
        P(("groups", "gx"), "gy"),
        P("groups", "gy", "gx"),
        P(("groups", "gy"), "gx"),
        P(),
        P(),
        P(),
        P(),
        P(),
    )
    return jax.shard_map(
        functools.partial(shards, mesh.shape["gx"], mesh.shape["gy"]),
        mesh=mesh,
        in_specs=placed,
        out_specs=(P("groups", "gx", "gy"), P("groups", "gy", "gx")),
        check_vma=False,
    )
```

```python
import functools

import jax
import jax.numpy as jnp
from jax import lax
from jax.experimental import pallas as pl
from jax.experimental.pallas import tpu as pltpu
from jax.sharding import PartitionSpec as P

diffuse = 0.08
vertical_mix = 0.1
time_step = 4.0
infiltrate = 0.5
evaporate = 1.0
storage = 0.1

LANES = 128
SUB = 8
MESH = pl.DeviceIdType.MESH
HIGH = lax.Precision.HIGHEST
F32 = jnp.float32


def dot(a, b):
    return jnp.dot(a, b, precision=HIGH, preferred_element_type=F32)


def dot_nt(a, b):
    return lax.dot_general(
        a, b, (((1,), (1,)), ((), ())), precision=HIGH, preferred_element_type=F32
    )


def each(count, body):
    if count <= 16:
        for index in range(count):
            body(index)
    else:

        @pl.loop(0, count)
        def _(index):
            body(index)


def turn(value, amount, axis):
    size = value.shape[axis]
    amount = amount % size
    return value if amount == 0 else pltpu.roll(value, amount, axis)


def retention(head, alpha, expo):
    expo_m = 1.0 - 1.0 / expo
    power = expo * jnp.log(alpha * jnp.abs(head))
    log_u = jnp.log(1.0 + jnp.exp(power))
    return power, log_u, expo_m, jnp.exp(-0.25 * expo_m * log_u)


def pick(kind, table_ref):
    value = jnp.full(kind.shape, table_ref[0], F32)
    for index in range(1, table_ref.shape[0]):
        value = jnp.where(kind == float(index), table_ref[index], value)
    return value


def kernel(
    ngx,
    ngy,
    theta_hbm,
    terrain_hbm,
    head_hbm,
    soil_hbm,
    tiles_hbm,
    pair_ref,
    alpha_ref,
    expo_ref,
    ksat_ref,
    done,
    head_out,
    th,
    sw,
    tr,
    hd,
    soil,
    soilf,
    tl,
    rowh,
    rows_soil,
    pack,
    colr,
    corner,
    gath,
    trs,
    trr,
    tcs,
    tcr,
    root,
    cap,
    diag,
    vec0,
    vec1,
    vec2,
    wvec,
    mom,
    momr,
    bsend,
    brecv,
    local_sem,
    near_send,
    near_recv,
    g_send,
    g_recv,
    t_send,
    t_recv,
    m_send,
    m_recv,
    b_send,
    b_recv,
):
    x = lax.axis_index("gx")
    y = lax.axis_index("gy")
    levs, height, width = head_hbm.shape
    lev, th_rows, _ = theta_hbm.shape
    tile_count = width // LANES
    nblock = gath.shape[0]
    ratio = height // 2 // th_rows
    group = ngx * ngy
    me = x * ngy + y
    ext_h, ext_w = height + SUB, width + LANES
    low, high_x = x > 0, x < ngx - 1
    left, right_y = y > 0, y < ngy - 1

    loads = []

    def load(src, dst):
        copy = pltpu.make_async_copy(src, dst, local_sem.at[len(loads)])
        copy.start()
        loads.append(copy)
        return copy

    c_theta = load(theta_hbm, th)
    c_head = load(head_hbm, hd.at[:, 0:height, 0:width])
    c_soil = load(soil_hbm, soil)
    c_terrain = load(terrain_hbm, tr)
    first = x * tile_count
    total_tiles = tiles_hbm.shape[0]
    tile_at = [
        jnp.minimum(jnp.maximum(first + i - 1, 0), total_tiles - 1)
        for i in range(tile_count + 2)
    ]
    c_tiles = [load(tiles_hbm.at[tile_at[i]], tl.at[i]) for i in range(tile_count + 2)]

    rowh[...] = jnp.zeros(rowh.shape, F32)
    rows_soil[...] = jnp.zeros(rows_soil.shape, jnp.int32)
    colr[...] = jnp.zeros(colr.shape, F32)
    corner[...] = jnp.zeros(corner.shape, F32)
    gath[...] = jnp.zeros(gath.shape, F32)
    trr[...] = jnp.zeros(trr.shape, F32)
    tcr[...] = jnp.zeros(tcr.shape, F32)

    barrier = pltpu.get_barrier_semaphore()

    def greet(index):
        @pl.when(index != me)
        def _():
            pl.semaphore_signal(
                barrier,
                inc=1,
                device_id={"gx": index // ngy, "gy": index % ngy},
                device_id_type=MESH,
            )

    each(group, greet)

    lane = lax.broadcasted_iota(jnp.int32, (1, LANES), 1)

    def pack_theta(sweep, source):
        trs[sweep, 0] = source[:, 0, :]
        trs[sweep, 1] = source[:, th_rows - 1, :]
        first_col = jnp.zeros((th_rows, LANES), F32)
        last_col = jnp.zeros((th_rows, LANES), F32)
        for k in range(lev):
            first_col = jnp.where(lane == k, turn(source[k], k, 1), first_col)
            last_col = jnp.where(lane == k, turn(source[k], k + 1, 1), last_col)
        tcs[sweep, 0] = first_col
        tcs[sweep, 1] = last_col

    c_theta.wait()
    pack_theta(0, th)

    c_head.wait()
    c_soil.wait()
    soilf[0:height, 0:width] = soil[...].astype(F32)
    edge_l = jnp.zeros((height, LANES), F32)
    edge_r = jnp.zeros((height, LANES), F32)
    for k in range(levs + 1):
        if k < levs:
            a, b = hd[k, 0:height, 0:LANES], hd[k, 0:height, width - LANES : width]
        else:
            a, b = soilf[0:height, 0:LANES], soilf[0:height, width - LANES : width]
        edge_l = jnp.where(lane // 4 == k, turn(a, 4 * k, 1), edge_l)
        edge_r = jnp.where((LANES - 1 - lane) // 4 == k, turn(b, -4 * k, 1), edge_r)
    pack[0] = edge_l
    pack[1] = edge_r

    pl.semaphore_wait(barrier, group - 1)

    sent = []

    def remote(src, dst, ssem, rsem, to):
        return pltpu.make_async_remote_copy(
            src_ref=src,
            dst_ref=dst,
            send_sem=ssem,
            recv_sem=rsem,
            device_id={"gx": to[0], "gy": to[1]},
            device_id_type=MESH,
        )

    def send(cond, *what):
        @pl.when(cond)
        def _():
            remote(*what).start()

        sent.append((cond, what))

    def arrive(cond, dst, rsem):
        @pl.when(cond)
        def _():
            remote(dst, dst, near_send.at[0], rsem, (x, y)).wait_recv()

    near = []

    def halo(index, cond, src, dst, to, cond_in):
        send(cond, src, dst, near_send.at[index], near_recv.at[index], to)
        near.append((cond_in, dst, near_recv.at[index]))

    halo(0, left, head_hbm.at[:, 0:SUB, :], rowh.at[0], (x, y - 1), right_y)
    halo(1, right_y, head_hbm.at[:, height - SUB :, :], rowh.at[1], (x, y + 1), left)
    halo(2, low, pack.at[0], colr.at[0], (x - 1, y), high_x)
    halo(3, high_x, pack.at[1], colr.at[1], (x + 1, y), low)

    dest = x // ratio
    part = x % ratio
    offset = pl.multiple_of(part * th_rows, th_rows)
    body = ratio * th_rows

    def spread(kind, cond, dest_y, src, dst, slot):
        def one(i):
            me_too = jnp.logical_and(i == x, dest_y == y)

            @pl.when(jnp.logical_and(cond, jnp.logical_not(me_too)))
            def _():
                remote(
                    src, dst, g_send.at[kind, i], g_recv.at[kind, slot], (i, dest_y)
                ).start()

        each(ngx, one)

        @pl.when(jnp.logical_and(cond, dest_y == y))
        def _():
            dst[...] = src[...]

        def finish(i):
            me_too = jnp.logical_and(i == x, dest_y == y)

            @pl.when(jnp.logical_and(cond, jnp.logical_not(me_too)))
            def _():
                remote(
                    src, dst, g_send.at[kind, i], g_recv.at[kind, slot], (i, dest_y)
                ).wait_send()

        return lambda: each(ngx, finish)

    slot = y * ratio + part
    at_first, at_last = part == 0, part == ratio - 1
    finish_spread = [
        spread(0, x >= 0, dest, th.at[0], gath.at[y, pl.ds(offset, th_rows)], slot),
        spread(
            1,
            jnp.logical_and(at_first, dest > 0),
            dest - 1,
            th.at[0, 0:SUB],
            gath.at[y, body : body + SUB],
            y,
        ),
        spread(
            2,
            jnp.logical_and(at_last, dest < ngy - 1),
            dest + 1,
            th.at[0, th_rows - SUB : th_rows],
            gath.at[y, body + SUB : body + 2 * SUB],
            y,
        ),
    ]

    halo(4, left, soil_hbm.at[0:SUB, :], rows_soil.at[0], (x, y - 1), right_y)
    halo(5, right_y, soil_hbm.at[height - SUB :, :], rows_soil.at[1], (x, y + 1), left)
    both = jnp.logical_and
    halo(6, both(low, left), pack.at[0, 0:SUB], corner.at[0], (x - 1, y - 1), both(high_x, right_y))
    halo(7, both(low, right_y), pack.at[0, height - SUB :], corner.at[1], (x - 1, y + 1), both(high_x, left))
    halo(8, both(high_x, left), pack.at[1, 0:SUB], corner.at[2], (x + 1, y - 1), both(low, right_y))
    halo(9, both(high_x, right_y), pack.at[1, height - SUB :], corner.at[3], (x + 1, y + 1), both(low, left))

    theta_in = []

    def theta_halo(sweep):
        got = []
        plan = (
            (low, trs, trr, 0, (x - 1, y), high_x),
            (high_x, trs, trr, 1, (x + 1, y), low),
            (left, tcs, tcr, 0, (x, y - 1), right_y),
            (right_y, tcs, tcr, 1, (x, y + 1), left),
        )
        for index, (cond, src, dst, side, to, cond_in) in enumerate(plan):
            send(
                cond,
                src.at[sweep, side],
                dst.at[sweep, side],
                t_send.at[sweep, index],
                t_recv.at[sweep, index],
                to,
            )
            got.append((cond_in, dst.at[sweep, side], t_recv.at[sweep, index]))
        theta_in.append(got)

    theta_halo(0)

    def state(k, rows, cols, alpha, expo, kmax, mask):
        power, log_u, expo_m, quarter = retention(hd[k, rows, cols], alpha, expo)
        sat = (quarter * quarter) * (quarter * quarter)
        cap[k, rows, cols] = (storage + sat) * (1.0 / time_step)
        value = jnp.sqrt(kmax) * quarter * (1.0 - jnp.exp(expo_m * (power - log_u)))
        root[k, rows, cols] = value if mask is None else jnp.where(mask, value, 0.0)

    def state_block(rows, cols, mask):
        kind = soilf[rows, cols]
        alpha, expo, kmax = (
            pick(kind, alpha_ref),
            pick(kind, expo_ref),
            pick(kind, ksat_ref),
        )
        for k in range(levs):
            state(k, rows, cols, alpha, expo, kmax, mask)

    for row in range(0, height, 32):
        state_block(slice(row, row + 32), slice(0, width), None)

    def sweep_once(sweep, source, store):
        for cond, dst, sem in theta_in[sweep]:
            arrive(cond, dst, sem)
        row_at = lax.broadcasted_iota(jnp.int32, (th_rows, LANES), 0)
        metric = diffuse * tr[...]
        from_right, from_left = tcr[sweep, 0], tcr[sweep, 1]
        for k in range(lev):
            centre = source[k]
            down = jnp.where(
                row_at == th_rows - 1, trr[sweep, 0, k : k + 1, :], turn(centre, -1, 0)
            )
            up = jnp.where(row_at == 0, trr[sweep, 1, k : k + 1, :], turn(centre, 1, 0))
            east = jnp.where(
                lane == LANES - 1, turn(from_right, LANES - 1 - k, 1), turn(centre, -1, 1)
            )
            west = jnp.where(lane == 0, turn(from_left, -k, 1), turn(centre, 1, 1))
            flat = down + up + east + west - 4.0 * centre
            vert = -2.0 * centre
            if k > 0:
                vert = vert + source[k - 1]
            if k < lev - 1:
                vert = vert + source[k + 1]
            store(k, centre + metric * flat + vertical_mix * vert)

    def store_first(k, value):
        sw[k] = value

    c_terrain.wait()
    sweep_once(0, th, store_first)
    pack_theta(1, sw)
    theta_halo(1)

    for cond, dst, sem in near:
        arrive(cond, dst, sem)
    upper = lax.broadcasted_iota(jnp.int32, (SUB, 1), 0) < 4
    first_half = lane < LANES // 2
    for k in range(levs):
        hd[k, height:ext_h, 0:width] = jnp.where(upper, rowh[0, k], rowh[1, k])
    soilf[height:ext_h, 0:width] = jnp.where(upper, rows_soil[0], rows_soil[1]).astype(F32)
    right_side, left_side = colr[0], colr[1]
    right_corner = jnp.where(upper, corner[0], corner[1])
    left_corner = jnp.where(upper, corner[2], corner[3])
    for k in range(levs + 1):
        side = jnp.where(first_half, turn(right_side, -4 * k, 1), turn(left_side, 4 * k, 1))
        tip = jnp.where(first_half, turn(right_corner, -4 * k, 1), turn(left_corner, 4 * k, 1))
        if k < levs:
            hd[k, 0:height, width:ext_w] = side
            hd[k, height:ext_h, width:ext_w] = tip
        else:
            soilf[0:height, width:ext_w] = side
            soilf[height:ext_h, width:ext_w] = tip

    col_ok = jnp.logical_or(
        jnp.logical_and(lane < 4, high_x), jnp.logical_and(lane >= LANES - 4, low)
    )
    row_ok = jnp.logical_or(
        jnp.logical_and(upper, right_y), jnp.logical_and(jnp.logical_not(upper), left)
    )
    state_block(
        slice(0, height), slice(width, ext_w), jnp.broadcast_to(col_ok, (height, LANES))
    )
    state_block(
        slice(height, ext_h), slice(0, width), jnp.broadcast_to(row_ok, (SUB, width))
    )
    state_block(
        slice(height, ext_h), slice(width, ext_w), jnp.logical_and(row_ok, col_ok)
    )

    def arrive_blocks(kind, cond, from_x, dst_of, slot_of):
        def one(b):
            mine = jnp.logical_and(from_x == x, b == y)

            @pl.when(jnp.logical_and(cond, jnp.logical_not(mine)))
            def _():
                dst = dst_of(b)
                remote(dst, dst, near_send.at[0], g_recv.at[kind, slot_of(b)], (x, y)).wait_recv()

        each(nblock, one)

    for r in range(ratio):
        arrive_blocks(
            0,
            x >= 0,
            y * ratio + r,
            lambda b, r=r: gath.at[b, r * th_rows : (r + 1) * th_rows],
            lambda b, r=r: b * ratio + r,
        )
    arrive_blocks(
        1, right_y, (y + 1) * ratio, lambda b: gath.at[b, body : body + SUB], lambda b: b
    )
    arrive_blocks(
        2,
        left,
        y * ratio - 1,
        lambda b: gath.at[b, body + SUB : body + 2 * SUB],
        lambda b: b,
    )
    for copy in c_tiles:
        copy.wait()
    grow_to = lax.broadcasted_iota(jnp.int32, (ext_h, body + 2 * SUB), 0)
    grow_from = lax.broadcasted_iota(jnp.int32, (ext_h, body + 2 * SUB), 1)
    source_row = jnp.where(
        grow_to < height + 4, grow_to // 2, body + 2 * SUB - 2 + (grow_to - height - 4) // 2
    )
    grow = jnp.where(grow_from == source_row, infiltrate, 0.0).astype(F32)

    def down(i):
        total = None
        for q in range(2):
            term = dot(gath[pair_ref[q, tile_at[i]]], tl[i, q])
            total = term if total is None else total + term
        return total

    infil = [dot(grow, down(i + 1)) for i in range(tile_count)]
    ends = jnp.where(first_half, down(tile_count + 1), down(0))
    infil.append(dot(grow, ends))

    def across(value):
        return (turn(value, 1, 1) + turn(value, -1, 1)) + (
            turn(value, 1, 0) + turn(value, -1, 0)
        )

    def around(ref, k):
        total = across(ref[k])
        if k > 0:
            total = total + ref[k - 1]
        if k < levs - 1:
            total = total + ref[k + 1]
        return total

    for k in range(levs):
        wvec[0, k] = root[k] * hd[k]
    for k in range(levs):
        centre = root[k]
        span = around(root, k)
        flow = around(wvec.at[0], k) - span * hd[k]
        if k > 0:
            flow = flow - root[k - 1]
        if k < levs - 1:
            flow = flow + root[k + 1]
        rhs = centre * flow
        if k == 0:
            rhs = rhs + jnp.concatenate(infil, axis=1)
        diag[k] = cap[k] + centre * span
        vec0[k] = rhs
        wvec[1, k] = centre * rhs

    def fold(value):
        part = None
        for c in range(0, width, LANES):
            for r in range(0, height, SUB):
                piece = value[r : r + SUB, c : c + LANES]
                part = piece if part is None else part + piece
        return part

    def plus(total, value):
        return value if total is None else total + value

    sums = [None] * 6
    for k in range(levs):
        here = vec0[k]
        image = diag[k] * here - root[k] * around(wvec.at[1], k)
        vec1[k] = image
        wvec[0, k] = root[k] * image
        sums[0] = plus(sums[0], fold(here * here))
        sums[1] = plus(sums[1], fold(here * image))
        sums[2] = plus(sums[2], fold(image * image))
    for k in range(levs):
        here = vec1[k]
        image = diag[k] * here - root[k] * around(wvec.at[0], k)
        vec2[k] = image
        wvec[1, k] = root[k] * image
        sums[3] = plus(sums[3], fold(here * image))
        sums[4] = plus(sums[4], fold(image * image))
    for k in range(levs):
        here = vec2[k]
        image = diag[k] * here - root[k] * around(wvec.at[1], k)
        sums[5] = plus(sums[5], fold(here * image))

    row8 = lax.broadcasted_iota(jnp.int32, (SUB, LANES), 0)
    packed = jnp.zeros((SUB, LANES), F32)
    for index, value in enumerate(sums):
        packed = jnp.where(row8 == index, jnp.sum(value, axis=0, keepdims=True), packed)
    mom[...] = packed
    momr[me] = packed

    def tell(index):
        @pl.when(index != me)
        def _():
            remote(
                mom, momr.at[me], m_send.at[index], m_recv.at[me], (index // ngy, index % ngy)
            ).start()

    each(group, tell)

    def store_second(k, value):
        done[k] = value

    sweep_once(1, sw, store_second)

    def hear(index):
        @pl.when(index != me)
        def _():
            remote(mom, momr.at[index], near_send.at[0], m_recv.at[index], (x, y)).wait_recv()

    each(group, hear)
    moments = jnp.sum(jnp.sum(momr[...], axis=0), axis=1, keepdims=True)
    mu = [moments[i : i + 1, :] for i in range(6)]
    scale = mu[1] / mu[0]
    inverse = mu[0] / mu[1]
    nu = []
    factor = 1.0 / mu[0]
    for i in range(6):
        nu.append(mu[i] * factor)
        factor = factor * inverse
    tiny = 1e-7
    l1, l2 = nu[2] / nu[1], nu[3] / nu[1]
    a11 = jnp.maximum(nu[3] - l1 * nu[2], tiny * nu[3])
    a12 = nu[4] - l1 * nu[3]
    b1 = nu[1] - l1 * nu[0]
    ratio_l = a12 / a11
    a22 = jnp.maximum(nu[5] - l2 * nu[3] - ratio_l * a12, tiny * nu[5])
    b2 = nu[2] - l2 * nu[0] - ratio_l * b1
    c2 = b2 / a22
    c1 = (b1 - a12 * c2) / a11
    c0 = (nu[0] - nu[2] * c1 - nu[3] * c2) / nu[1]
    c0 = c0 * inverse
    c1 = c1 * inverse * inverse
    c2 = c2 * inverse * inverse * inverse

    def advance_head(k):
        own = (k, slice(0, height), slice(0, width))
        value = hd[own] + (c0 * vec0[own] + c1 * vec1[own] + c2 * vec2[own])
        head_out[k] = value
        return value

    surface = advance_head(0)
    kind = soilf[0:height, 0:width]
    _, _, _, quarter = retention(surface, pick(kind, alpha_ref), pick(kind, expo_ref))
    moist = (quarter * quarter) * (quarter * quarter)
    pair_row = lax.broadcasted_iota(jnp.int32, (body, height), 0)
    pair_col = lax.broadcasted_iota(jnp.int32, (body, height), 1)
    halver = jnp.where(pair_col // 2 == pair_row, 0.5, 0.0).astype(F32)
    halves = dot(halver, moist)
    contrib = []
    for i in range(tile_count):
        for q in range(2):
            contrib.append(
                (
                    pair_ref[q, first + i],
                    dot_nt(halves[:, i * LANES : (i + 1) * LANES], tl[i + 1, q]),
                )
            )

    for t in range(nblock):
        total = jnp.zeros((body, LANES), F32)
        for where_to, value in contrib:
            total = total + jnp.where(where_to == t, value, 0.0)
        for r in range(ratio):
            piece = total[r * th_rows : (r + 1) * th_rows]
            bsend[t * ratio + r] = piece
            to_x = y * ratio + r
            mine = jnp.logical_and(to_x == x, y == t)

            @pl.when(mine)
            def _():
                brecv[x] = piece

            @pl.when(jnp.logical_not(mine))
            def _():
                remote(
                    bsend.at[t * ratio + r],
                    brecv.at[x],
                    b_send.at[t * ratio + r],
                    b_recv.at[x],
                    (to_x, t),
                ).start()

    for k in range(1, levs):
        advance_head(k)

    own_y = x // ratio

    def collect(index):
        mine = jnp.logical_and(index == x, own_y == y)

        @pl.when(jnp.logical_not(mine))
        def _():
            remote(
                brecv.at[index], brecv.at[index], near_send.at[0], b_recv.at[index], (x, y)
            ).wait_recv()

    each(ngx, collect)
    done[0] = done[0] + evaporate * jnp.sum(brecv[...], axis=0)

    for cond, what in sent:

        @pl.when(cond)
        def _():
            remote(*what).wait_send()

    for finish in finish_spread:
        finish()

    def told(index):
        @pl.when(index != me)
        def _():
            remote(
                mom, momr.at[me], m_send.at[index], m_recv.at[me], (index // ngy, index % ngy)
            ).wait_send()

    each(group, told)
    for t in range(nblock):
        for r in range(ratio):
            to_x = y * ratio + r

            @pl.when(jnp.logical_not(jnp.logical_and(to_x == x, y == t)))
            def _():
                remote(
                    bsend.at[t * ratio + r],
                    brecv.at[x],
                    b_send.at[t * ratio + r],
                    b_recv.at[x],
                    (to_x, t),
                ).wait_send()


def deliver(theta_ref, head_ref, theta_out, head_out, sem):
    copies = [
        pltpu.make_async_copy(theta_ref, theta_out, sem.at[0]),
        pltpu.make_async_copy(head_ref, head_out, sem.at[1]),
    ]
    for copy in copies:
        copy.start()
    for copy in copies:
        copy.wait()


def shards(ngx, ngy, theta, terrain, head, soil, pair_map, tiles, vg_alpha, vg_n, ksat):
    lev, th_rows, _ = theta.shape
    levs, height, width = head.shape
    body = height // 2
    ratio = body // th_rows
    tile_count = width // LANES
    ext = (levs, height + SUB, width + LANES)
    dma = pltpu.SemaphoreType.DMA
    group = ngx * ngy
    anywhere = pl.BlockSpec(memory_space=pltpu.HBM)
    whole = pl.BlockSpec(memory_space=pltpu.VMEM)
    scalars = pl.BlockSpec(memory_space=pltpu.SMEM)
    vmem = lambda *shape: pltpu.VMEM(shape, F32)
    results = pl.pallas_call(
        functools.partial(kernel, ngx, ngy),
        out_shape=(
            jax.ShapeDtypeStruct(theta.shape, F32),
            jax.ShapeDtypeStruct(head.shape, F32),
        ),
        in_specs=[anywhere] * 5 + [scalars] * 4,
        out_specs=(whole, whole),
        scratch_shapes=[
            vmem(*theta.shape),
            vmem(*theta.shape),
            vmem(*terrain.shape),
            vmem(*ext),
            pltpu.VMEM((height, width), jnp.int32),
            vmem(*ext[1:]),
            vmem(tile_count + 2, 2, LANES, LANES),
            vmem(2, levs, SUB, width),
            pltpu.VMEM((2, SUB, width), jnp.int32),
            vmem(2, height, LANES),
            vmem(2, height, LANES),
            vmem(4, SUB, LANES),
            vmem(ngy, body + 2 * SUB, LANES),
            vmem(2, 2, lev, LANES),
            vmem(2, 2, lev, LANES),
            vmem(2, 2, th_rows, LANES),
            vmem(2, 2, th_rows, LANES),
            vmem(*ext),
            vmem(*ext),
            vmem(*ext),
            vmem(*ext),
            vmem(*ext),
            vmem(*ext),
            vmem(2, *ext),
            vmem(SUB, LANES),
            vmem(group, SUB, LANES),
            vmem(ngy * ratio, th_rows, LANES),
            vmem(ngx, th_rows, LANES),
            dma((tile_count + 6,)),
            dma((10,)),
            dma((10,)),
            dma((3, ngx)),
            dma((3, ngy * ratio)),
            dma((2, 4)),
            dma((2, 4)),
            dma((group,)),
            dma((group,)),
            dma((ngy * ratio,)),
            dma((ngx,)),
        ],
        compiler_params=pltpu.CompilerParams(
            collective_id=0, has_side_effects=True, vmem_limit_bytes=63 * 1024 * 1024
        ),
        name="coupled_step",
    )(theta, terrain, head, soil, tiles, pair_map.T, vg_alpha, vg_n, ksat)
    anyplace = pl.BlockSpec(memory_space=pl.ANY)
    return pl.pallas_call(
        deliver,
        out_shape=tuple(jax.ShapeDtypeStruct(r.shape, F32) for r in results),
        in_specs=[anyplace, anyplace],
        out_specs=(anywhere, anywhere),
        scratch_shapes=[dma((2,))],
        compiler_params=pltpu.CompilerParams(vmem_limit_bytes=63 * 1024 * 1024),
        name="deliver",
    )(*results)


def solution(mesh):
    placed = (
        P("groups", "gx", "gy"),
        P(("groups", "gx"), "gy"),
        P("groups", "gy", "gx"),
        P(("groups", "gy"), "gx"),
        P(),
        P(),
        P(),
        P(),
        P(),
    )
    return jax.shard_map(
        functools.partial(shards, mesh.shape["gx"], mesh.shape["gy"]),
        mesh=mesh,
        in_specs=placed,
        out_specs=(P("groups", "gx", "gy"), P("groups", "gy", "gx")),
        check_vma=False,
    )
```

```python
import functools

import jax
import jax.numpy as jnp
from jax import lax
from jax.experimental import pallas as pl
from jax.experimental.pallas import tpu as pltpu
from jax.sharding import PartitionSpec as P

diffuse = 0.08
vertical_mix = 0.1
time_step = 4.0
infiltrate = 0.5
evaporate = 1.0
storage = 0.1

LANES = 128
SUB = 8
MESH = pl.DeviceIdType.MESH
HIGH = lax.Precision.HIGHEST
F32 = jnp.float32


def dot(a, b):
    return jnp.dot(a, b, precision=HIGH, preferred_element_type=F32)


def dot_nt(a, b):
    return lax.dot_general(
        a, b, (((1,), (1,)), ((), ())), precision=HIGH, preferred_element_type=F32
    )


def each(count, body):
    if count <= 16:
        for index in range(count):
            body(index)
    else:

        @pl.loop(0, count)
        def _(index):
            body(index)


def turn(value, amount, axis):
    size = value.shape[axis]
    amount = amount % size
    return value if amount == 0 else pltpu.roll(value, amount, axis)


def retention(head, alpha, expo):
    expo_m = 1.0 - 1.0 / expo
    power = expo * jnp.log(alpha * jnp.abs(head))
    log_u = jnp.log(1.0 + jnp.exp(power))
    return power, log_u, expo_m, jnp.exp(-0.25 * expo_m * log_u)


def pick(kind, table_ref):
    value = jnp.full(kind.shape, table_ref[0], F32)
    for index in range(1, table_ref.shape[0]):
        value = jnp.where(kind == float(index), table_ref[index], value)
    return value


def kernel(
    ngx,
    ngy,
    theta_hbm,
    terrain_hbm,
    head_hbm,
    soil_hbm,
    tiles_hbm,
    pair_ref,
    alpha_ref,
    expo_ref,
    ksat_ref,
    theta_out,
    head_out,
    th,
    sw,
    done,
    tr,
    hd,
    soil,
    soilf,
    tl,
    rows_out,
    rows_in,
    cols_out,
    cols_in,
    corner,
    gath,
    edge_out,
    edge_in,
    trs,
    trr,
    tcs,
    tcr,
    root,
    cap,
    diag,
    vec0,
    vec1,
    vec2,
    wvec,
    mom,
    momr,
    bsend,
    brecv,
    local_sem,
    out_sem,
    near_send,
    near_recv,
    g_send,
    g_recv,
    t_send,
    t_recv,
    m_send,
    m_recv,
    b_send,
    b_recv,
):
    x = lax.axis_index("gx")
    y = lax.axis_index("gy")
    levs, height, width = head_hbm.shape
    lev, th_rows, _ = theta_hbm.shape
    tile_count = width // LANES
    nblock = gath.shape[0]
    ratio = height // 2 // th_rows
    group = ngx * ngy
    me = x * ngy + y
    ext_h, ext_w = height + SUB, width + LANES
    low, high_x = x > 0, x < ngx - 1
    left, right_y = y > 0, y < ngy - 1

    loads = []

    def load(src, dst):
        copy = pltpu.make_async_copy(src, dst, local_sem.at[len(loads)])
        copy.start()
        loads.append(copy)
        return copy

    c_theta = load(theta_hbm, th)
    c_head = load(head_hbm, hd.at[:, 0:height, 0:width])
    c_soil = load(soil_hbm, soil)
    c_terrain = load(terrain_hbm, tr)
    first = x * tile_count
    total_tiles = tiles_hbm.shape[0]
    tile_at = [
        jnp.minimum(jnp.maximum(first + i - 1, 0), total_tiles - 1)
        for i in range(tile_count + 2)
    ]
    c_tiles = [load(tiles_hbm.at[tile_at[i]], tl.at[i]) for i in range(tile_count + 2)]

    rows_in[...] = jnp.zeros(rows_in.shape, F32)
    cols_in[...] = jnp.zeros(cols_in.shape, F32)
    corner[...] = jnp.zeros(corner.shape, F32)
    edge_in[...] = jnp.zeros(edge_in.shape, F32)
    trr[...] = jnp.zeros(trr.shape, F32)
    tcr[...] = jnp.zeros(tcr.shape, F32)

    barrier = pltpu.get_barrier_semaphore()

    def greet(index):
        @pl.when(index != me)
        def _():
            pl.semaphore_signal(
                barrier,
                inc=1,
                device_id={"gx": index // ngy, "gy": index % ngy},
                device_id_type=MESH,
            )

    each(group, greet)

    lane = lax.broadcasted_iota(jnp.int32, (1, LANES), 1)

    def edge_columns(source):
        first_col = jnp.zeros((th_rows, LANES), F32)
        last_col = jnp.zeros((th_rows, LANES), F32)
        for k in range(lev):
            first_col = jnp.where(lane == k, turn(source[k], k, 1), first_col)
            last_col = jnp.where(lane == k, turn(source[k], k + 1, 1), last_col)
        return first_col, last_col

    def place(chunk):
        col = (chunk % tile_count) * LANES
        return levs + 1 + chunk // tile_count, slice(0, SUB), slice(col, col + LANES)

    c_theta.wait()
    cols_out[0, height:] = th[:, 0, :]
    cols_out[1, height:] = th[:, th_rows - 1, :]
    for side, columns in enumerate(edge_columns(th)):
        for chunk in range(th_rows // SUB):
            rows_out[(side,) + place(chunk)] = columns[chunk * SUB : (chunk + 1) * SUB]

    c_head.wait()
    c_soil.wait()
    soilf[0:height, 0:width] = soil[...].astype(F32)
    edge_l = jnp.zeros((height, LANES), F32)
    edge_r = jnp.zeros((height, LANES), F32)
    for k in range(levs + 1):
        if k < levs:
            a, b = hd[k, 0:height, 0:LANES], hd[k, 0:height, width - LANES : width]
        else:
            a, b = soilf[0:height, 0:LANES], soilf[0:height, width - LANES : width]
        edge_l = jnp.where(lane // 4 == k, turn(a, 4 * k, 1), edge_l)
        edge_r = jnp.where((LANES - 1 - lane) // 4 == k, turn(b, -4 * k, 1), edge_r)
    cols_out[0, 0:height] = edge_l
    cols_out[1, 0:height] = edge_r
    for side, row in enumerate((0, height - SUB)):
        rows_out[side, 0:levs] = hd[:, row : row + SUB, 0:width]
        rows_out[side, levs] = soilf[row : row + SUB, 0:width]

    pl.semaphore_wait(barrier, group - 1)

    sent = []

    def remote(src, dst, ssem, rsem, to):
        return pltpu.make_async_remote_copy(
            src_ref=src,
            dst_ref=dst,
            send_sem=ssem,
            recv_sem=rsem,
            device_id={"gx": to[0], "gy": to[1]},
            device_id_type=MESH,
        )

    def send(cond, *what):
        @pl.when(cond)
        def _():
            remote(*what).start()

        sent.append((cond, what))

    def arrive(cond, dst, rsem):
        @pl.when(cond)
        def _():
            remote(dst, dst, near_send.at[0], rsem, (x, y)).wait_recv()

    near = []

    def halo(index, cond, src, dst, to, cond_in):
        send(cond, src, dst, near_send.at[index], near_recv.at[index], to)
        near.append((cond_in, dst, near_recv.at[index]))

    both = jnp.logical_and
    halo(0, left, rows_out.at[0], rows_in.at[0], (x, y - 1), right_y)
    halo(1, right_y, rows_out.at[1], rows_in.at[1], (x, y + 1), left)
    halo(2, low, cols_out.at[0], cols_in.at[0], (x - 1, y), high_x)
    halo(3, high_x, cols_out.at[1], cols_in.at[1], (x + 1, y), low)

    dest = x // ratio
    part = x % ratio
    offset = pl.multiple_of(part * th_rows, th_rows)
    body = ratio * th_rows

    slot = y * ratio + part
    src, dst = th.at[0], gath.at[y, pl.ds(offset, th_rows)]

    def spread(act):
        def one(i):
            @pl.when(jnp.logical_not(both(i == x, dest == y)))
            def _():
                act(remote(src, dst, g_send.at[i], g_recv.at[slot], (i, dest)))

        each(ngx, one)

    spread(lambda copy: copy.start())

    @pl.when(dest == y)
    def _():
        dst[...] = src[...]

    halo(4, both(low, left), cols_out.at[0, 0:SUB], corner.at[0], (x - 1, y - 1), both(high_x, right_y))
    halo(5, both(low, right_y), cols_out.at[0, height - SUB : height], corner.at[1], (x - 1, y + 1), both(high_x, left))
    halo(6, both(high_x, left), cols_out.at[1, 0:SUB], corner.at[2], (x + 1, y - 1), both(low, right_y))
    halo(7, both(high_x, right_y), cols_out.at[1, height - SUB : height], corner.at[3], (x + 1, y + 1), both(low, left))

    theta_in = []

    def theta_halo():
        plan = (
            (low, trs, trr, 0, (x - 1, y), high_x),
            (high_x, trs, trr, 1, (x + 1, y), low),
            (left, tcs, tcr, 0, (x, y - 1), right_y),
            (right_y, tcs, tcr, 1, (x, y + 1), left),
        )
        for index, (cond, src, dst, side, to, cond_in) in enumerate(plan):
            send(cond, src.at[side], dst.at[side], t_send.at[index], t_recv.at[index], to)
            theta_in.append((cond_in, dst.at[side], t_recv.at[index]))

    def state(k, rows, cols, alpha, expo, kmax, mask):
        power, log_u, expo_m, quarter = retention(hd[k, rows, cols], alpha, expo)
        sat = (quarter * quarter) * (quarter * quarter)
        cap[k, rows, cols] = (storage + sat) * (1.0 / time_step)
        value = jnp.sqrt(kmax) * quarter * (1.0 - jnp.exp(expo_m * (power - log_u)))
        root[k, rows, cols] = value if mask is None else jnp.where(mask, value, 0.0)

    def state_block(rows, cols, mask):
        kind = soilf[rows, cols]
        alpha, expo, kmax = (
            pick(kind, alpha_ref),
            pick(kind, expo_ref),
            pick(kind, ksat_ref),
        )
        for k in range(levs):
            state(k, rows, cols, alpha, expo, kmax, mask)

    for row in range(0, height, 32):
        state_block(slice(row, row + 32), slice(0, width), None)

    def sweep_once(source, row_below, row_above, from_right, from_left, store):
        row_at = lax.broadcasted_iota(jnp.int32, (th_rows, LANES), 0)
        metric = diffuse * tr[...]
        for k in range(lev):
            centre = source[k]
            down = jnp.where(
                row_at == th_rows - 1, row_below(k), turn(centre, -1, 0)
            )
            up = jnp.where(row_at == 0, row_above(k), turn(centre, 1, 0))
            east = jnp.where(
                lane == LANES - 1, turn(from_right, LANES - 1 - k, 1), turn(centre, -1, 1)
            )
            west = jnp.where(lane == 0, turn(from_left, -k, 1), turn(centre, 1, 1))
            flat = down + up + east + west - 4.0 * centre
            vert = -2.0 * centre
            if k > 0:
                vert = vert + source[k - 1]
            if k < lev - 1:
                vert = vert + source[k + 1]
            store(k, centre + metric * flat + vertical_mix * vert)

    def store_first(k, value):
        sw[k] = value

    first_half = lane < LANES // 2
    for r in range(ratio):

        def one(b, r=r):
            @pl.when(jnp.logical_not(both(y * ratio + r == x, b == y)))
            def _():
                arrived = gath.at[b, r * th_rows : (r + 1) * th_rows]
                remote(
                    arrived, arrived, near_send.at[0], g_recv.at[b * ratio + r], (x, y)
                ).wait_recv()

        each(nblock, one)
    for copy in c_tiles:
        copy.wait()
    grow_to = lax.broadcasted_iota(jnp.int32, (height, body), 0)
    grow_from = lax.broadcasted_iota(jnp.int32, (height, body), 1)
    grow = jnp.where(grow_from == grow_to // 2, infiltrate, 0.0).astype(F32)

    def down(i):
        total = None
        for q in range(2):
            term = dot(gath[pair_ref[q, tile_at[i]]], tl[i, q])
            total = term if total is None else total + term
        return total

    blocks = [down(i + 1) for i in range(tile_count)]
    blocks.append(jnp.where(first_half, down(tile_count + 1), down(0)))
    infil = dot(grow, jnp.concatenate(blocks, axis=1))
    edge_out[0] = infil[0:SUB]
    edge_out[1] = infil[height - SUB : height]
    vec0[0, 0:height] = infil
    edges_here = len(near)
    halo(8, left, edge_out.at[0], edge_in.at[0], (x, y - 1), right_y)
    halo(9, right_y, edge_out.at[1], edge_in.at[1], (x, y + 1), left)

    for cond, dst, sem in near[:edges_here]:
        arrive(cond, dst, sem)
    upper = lax.broadcasted_iota(jnp.int32, (SUB, 1), 0) < 4
    for k in range(levs):
        hd[k, height:ext_h, 0:width] = jnp.where(upper, rows_in[0, k], rows_in[1, k])
    soilf[height:ext_h, 0:width] = jnp.where(upper, rows_in[0, levs], rows_in[1, levs])
    right_side, left_side = cols_in[0, 0:height], cols_in[1, 0:height]
    right_corner = jnp.where(upper, corner[0], corner[1])
    left_corner = jnp.where(upper, corner[2], corner[3])
    for k in range(levs + 1):
        side = jnp.where(first_half, turn(right_side, -4 * k, 1), turn(left_side, 4 * k, 1))
        tip = jnp.where(first_half, turn(right_corner, -4 * k, 1), turn(left_corner, 4 * k, 1))
        if k < levs:
            hd[k, 0:height, width:ext_w] = side
            hd[k, height:ext_h, width:ext_w] = tip
        else:
            soilf[0:height, width:ext_w] = side
            soilf[height:ext_h, width:ext_w] = tip

    col_ok = jnp.logical_or(
        jnp.logical_and(lane < 4, high_x), jnp.logical_and(lane >= LANES - 4, low)
    )
    row_ok = jnp.logical_or(
        jnp.logical_and(upper, right_y), jnp.logical_and(jnp.logical_not(upper), left)
    )
    state_block(
        slice(0, height), slice(width, ext_w), jnp.broadcast_to(col_ok, (height, LANES))
    )
    state_block(
        slice(height, ext_h), slice(0, width), jnp.broadcast_to(row_ok, (SUB, width))
    )
    state_block(
        slice(height, ext_h), slice(width, ext_w), jnp.logical_and(row_ok, col_ok)
    )

    def store_first(k, value):
        sw[k] = value

    def edge_column(side):
        pieces = [rows_in[(side,) + place(chunk)] for chunk in range(th_rows // SUB)]
        return jnp.concatenate(pieces, axis=0)

    c_terrain.wait()
    sweep_once(
        th,
        lambda k: cols_in[0, height + k : height + k + 1],
        lambda k: cols_in[1, height + k : height + k + 1],
        edge_column(0),
        edge_column(1),
        store_first,
    )
    trs[0] = sw[:, 0, :]
    trs[1] = sw[:, th_rows - 1, :]
    tcs[0], tcs[1] = edge_columns(sw)
    theta_halo()

    def across(value):
        return (turn(value, 1, 1) + turn(value, -1, 1)) + (
            turn(value, 1, 0) + turn(value, -1, 0)
        )

    def around(ref, k):
        total = across(ref[k])
        if k > 0:
            total = total + ref[k - 1]
        if k < levs - 1:
            total = total + ref[k + 1]
        return total

    for k in range(levs):
        wvec[0, k] = root[k] * hd[k]
    for k in reversed(range(levs)):
        centre = root[k]
        span = around(root, k)
        flow = around(wvec.at[0], k) - span * hd[k]
        if k > 0:
            flow = flow - root[k - 1]
        if k < levs - 1:
            flow = flow + root[k + 1]
        rhs = centre * flow
        if k == 0:
            for cond, dst, sem in near[edges_here:]:
                arrive(cond, dst, sem)
            edge = jnp.where(upper, edge_in[0], edge_in[1])
            rhs = rhs + jnp.concatenate([vec0[0, 0:height], edge], axis=0)
        diag[k] = cap[k] + centre * span
        vec0[k] = rhs
        wvec[1, k] = centre * rhs

    def fold(value):
        part = None
        for c in range(0, width, LANES):
            for r in range(0, height, SUB):
                piece = value[r : r + SUB, c : c + LANES]
                part = piece if part is None else part + piece
        return part

    def plus(total, value):
        return value if total is None else total + value

    sums = [None] * 6
    for k in range(levs):
        here = vec0[k]
        image = diag[k] * here - root[k] * around(wvec.at[1], k)
        vec1[k] = image
        wvec[0, k] = root[k] * image
        sums[0] = plus(sums[0], fold(here * here))
        sums[1] = plus(sums[1], fold(here * image))
        sums[2] = plus(sums[2], fold(image * image))
    for k in range(levs):
        here = vec1[k]
        image = diag[k] * here - root[k] * around(wvec.at[0], k)
        vec2[k] = image
        wvec[1, k] = root[k] * image
        sums[3] = plus(sums[3], fold(here * image))
        sums[4] = plus(sums[4], fold(image * image))
    for k in range(levs):
        here = vec2[k]
        image = diag[k] * here - root[k] * around(wvec.at[1], k)
        sums[5] = plus(sums[5], fold(here * image))

    row8 = lax.broadcasted_iota(jnp.int32, (SUB, LANES), 0)
    packed = jnp.zeros((SUB, LANES), F32)
    for index, value in enumerate(sums):
        packed = jnp.where(row8 == index, jnp.sum(value, axis=0, keepdims=True), packed)
    mom[...] = packed
    momr[me] = packed

    def tell(index):
        @pl.when(index != me)
        def _():
            remote(
                mom, momr.at[me], m_send.at[index], m_recv.at[me], (index // ngy, index % ngy)
            ).start()

    each(group, tell)

    for cond, what in sent:

        @pl.when(cond)
        def _():
            remote(*what).wait_send()

    spread(lambda copy: copy.wait_send())
    for cond, dst, sem in theta_in:
        arrive(cond, dst, sem)

    def store_second(k, value):
        done[k] = value

    sweep_once(
        sw,
        lambda k: trr[0, k : k + 1],
        lambda k: trr[1, k : k + 1],
        tcr[0],
        tcr[1],
        store_second,
    )
    out_theta = pltpu.make_async_copy(done.at[1:lev], theta_out.at[1:lev], out_sem.at[0])
    out_theta.start()

    def hear(index):
        @pl.when(index != me)
        def _():
            remote(mom, momr.at[index], near_send.at[0], m_recv.at[index], (x, y)).wait_recv()

    each(group, hear)
    moments = jnp.sum(jnp.sum(momr[...], axis=0), axis=1, keepdims=True)
    mu = [moments[i : i + 1, :] for i in range(6)]
    scale = mu[1] / mu[0]
    inverse = mu[0] / mu[1]
    nu = []
    factor = 1.0 / mu[0]
    for i in range(6):
        nu.append(mu[i] * factor)
        factor = factor * inverse
    tiny = 1e-7
    l1, l2 = nu[2] / nu[1], nu[3] / nu[1]
    a11 = jnp.maximum(nu[3] - l1 * nu[2], tiny * nu[3])
    a12 = nu[4] - l1 * nu[3]
    b1 = nu[1] - l1 * nu[0]
    ratio_l = a12 / a11
    a22 = jnp.maximum(nu[5] - l2 * nu[3] - ratio_l * a12, tiny * nu[5])
    b2 = nu[2] - l2 * nu[0] - ratio_l * b1
    c2 = b2 / a22
    c1 = (b1 - a12 * c2) / a11
    c0 = (nu[0] - nu[2] * c1 - nu[3] * c2) / nu[1]
    c0 = c0 * inverse
    c1 = c1 * inverse * inverse
    c2 = c2 * inverse * inverse * inverse

    def advance_head(k):
        own = (k, slice(0, height), slice(0, width))
        value = hd[own] + (c0 * vec0[own] + c1 * vec1[own] + c2 * vec2[own])
        hd[own] = value
        return value

    surface = advance_head(0)
    kind = soilf[0:height, 0:width]
    _, _, _, quarter = retention(surface, pick(kind, alpha_ref), pick(kind, expo_ref))
    moist = (quarter * quarter) * (quarter * quarter)
    pair_row = lax.broadcasted_iota(jnp.int32, (body, height), 0)
    pair_col = lax.broadcasted_iota(jnp.int32, (body, height), 1)
    halver = jnp.where(pair_col // 2 == pair_row, 0.5, 0.0).astype(F32)
    halves = dot(halver, moist)
    contrib = []
    for i in range(tile_count):
        for q in range(2):
            contrib.append(
                (
                    pair_ref[q, first + i],
                    dot_nt(halves[:, i * LANES : (i + 1) * LANES], tl[i + 1, q]),
                )
            )

    for t in range(nblock):
        total = jnp.zeros((body, LANES), F32)
        for where_to, value in contrib:
            total = total + jnp.where(where_to == t, value, 0.0)
        for r in range(ratio):
            piece = total[r * th_rows : (r + 1) * th_rows]
            bsend[t * ratio + r] = piece
            to_x = y * ratio + r
            mine = jnp.logical_and(to_x == x, y == t)

            @pl.when(mine)
            def _():
                brecv[x] = piece

            @pl.when(jnp.logical_not(mine))
            def _():
                remote(
                    bsend.at[t * ratio + r],
                    brecv.at[x],
                    b_send.at[t * ratio + r],
                    b_recv.at[x],
                    (to_x, t),
                ).start()

    for k in range(1, levs):
        advance_head(k)

    out_head = pltpu.make_async_copy(hd.at[:, 0:height, 0:width], head_out, out_sem.at[1])
    out_head.start()

    def told(index):
        @pl.when(index != me)
        def _():
            remote(
                mom, momr.at[me], m_send.at[index], m_recv.at[me], (index // ngy, index % ngy)
            ).wait_send()

    each(group, told)

    own_y = x // ratio

    def collect(index):
        mine = jnp.logical_and(index == x, own_y == y)

        @pl.when(jnp.logical_not(mine))
        def _():
            remote(
                brecv.at[index], brecv.at[index], near_send.at[0], b_recv.at[index], (x, y)
            ).wait_recv()

    each(ngx, collect)
    done[0] = done[0] + evaporate * jnp.sum(brecv[...], axis=0)

    out_level = pltpu.make_async_copy(done.at[0], theta_out.at[0], out_sem.at[2])
    out_level.start()
    for t in range(nblock):
        for r in range(ratio):
            to_x = y * ratio + r

            @pl.when(jnp.logical_not(jnp.logical_and(to_x == x, y == t)))
            def _():
                remote(
                    bsend.at[t * ratio + r],
                    brecv.at[x],
                    b_send.at[t * ratio + r],
                    b_recv.at[x],
                    (to_x, t),
                ).wait_send()

    out_theta.wait()
    out_head.wait()
    out_level.wait()


def shards(ngx, ngy, theta, terrain, head, soil, pair_map, tiles, vg_alpha, vg_n, ksat):
    lev, th_rows, _ = theta.shape
    levs, height, width = head.shape
    body = height // 2
    ratio = body // th_rows
    tile_count = width // LANES
    slabs = levs + 1 + pl.cdiv(th_rows // SUB, tile_count)
    ext = (levs, height + SUB, width + LANES)
    dma = pltpu.SemaphoreType.DMA
    group = ngx * ngy
    anywhere = pl.BlockSpec(memory_space=pltpu.HBM)
    scalars = pl.BlockSpec(memory_space=pltpu.SMEM)
    vmem = lambda *shape: pltpu.VMEM(shape, F32)
    return pl.pallas_call(
        functools.partial(kernel, ngx, ngy),
        out_shape=(
            jax.ShapeDtypeStruct(theta.shape, F32),
            jax.ShapeDtypeStruct(head.shape, F32),
        ),
        in_specs=[anywhere] * 5 + [scalars] * 4,
        out_specs=(anywhere, anywhere),
        scratch_shapes=[
            vmem(*theta.shape),
            vmem(*theta.shape),
            vmem(*theta.shape),
            vmem(*terrain.shape),
            vmem(*ext),
            pltpu.VMEM((height, width), jnp.int32),
            vmem(*ext[1:]),
            vmem(tile_count + 2, 2, LANES, LANES),
            vmem(2, slabs, SUB, width),
            vmem(2, slabs, SUB, width),
            vmem(2, height + lev, LANES),
            vmem(2, height + lev, LANES),
            vmem(4, SUB, LANES),
            vmem(ngy, body, LANES),
            vmem(2, SUB, width + LANES),
            vmem(2, SUB, width + LANES),
            vmem(2, lev, LANES),
            vmem(2, lev, LANES),
            vmem(2, th_rows, LANES),
            vmem(2, th_rows, LANES),
            vmem(*ext),
            vmem(*ext),
            vmem(*ext),
            vmem(*ext),
            vmem(*ext),
            vmem(*ext),
            vmem(2, *ext),
            vmem(SUB, LANES),
            vmem(group, SUB, LANES),
            vmem(ngy * ratio, th_rows, LANES),
            vmem(ngx, th_rows, LANES),
            dma((tile_count + 6,)),
            dma((3,)),
            dma((10,)),
            dma((10,)),
            dma((ngx,)),
            dma((ngy * ratio,)),
            dma((4,)),
            dma((4,)),
            dma((group,)),
            dma((group,)),
            dma((ngy * ratio,)),
            dma((ngx,)),
        ],
        compiler_params=pltpu.CompilerParams(
            collective_id=0, has_side_effects=True, vmem_limit_bytes=63 * 1024 * 1024
        ),
        name="coupled_step",
    )(theta, terrain, head, soil, tiles, pair_map.T, vg_alpha, vg_n, ksat)


def solution(mesh):
    placed = (
        P("groups", "gx", "gy"),
        P(("groups", "gx"), "gy"),
        P("groups", "gy", "gx"),
        P(("groups", "gy"), "gx"),
        P(),
        P(),
        P(),
        P(),
        P(),
    )
    return jax.shard_map(
        functools.partial(shards, mesh.shape["gx"], mesh.shape["gy"]),
        mesh=mesh,
        in_specs=placed,
        out_specs=(P("groups", "gx", "gy"), P("groups", "gy", "gx")),
        check_vma=False,
    )
```

```python
import functools

import jax
import jax.numpy as jnp
from jax import lax
from jax.experimental import pallas as pl
from jax.experimental.pallas import tpu as pltpu
from jax.sharding import PartitionSpec as P

diffuse = 0.08
vertical_mix = 0.1
time_step = 4.0
infiltrate = 0.5
evaporate = 1.0
storage = 0.1

LANES = 128
SUB = 8
MESH = pl.DeviceIdType.MESH
HIGH = lax.Precision.HIGHEST
F32 = jnp.float32


def dot(a, b):
    return jnp.dot(a, b, precision=HIGH, preferred_element_type=F32)


def dot_nt(a, b):
    return lax.dot_general(
        a, b, (((1,), (1,)), ((), ())), precision=HIGH, preferred_element_type=F32
    )


def each(count, body):
    if count <= 16:
        for index in range(count):
            body(index)
    else:

        @pl.loop(0, count)
        def _(index):
            body(index)


def turn(value, amount, axis):
    size = value.shape[axis]
    amount = amount % size
    return value if amount == 0 else pltpu.roll(value, amount, axis)


def retention(head, alpha, expo):
    expo_m = 1.0 - 1.0 / expo
    power = expo * jnp.log(alpha * jnp.abs(head))
    log_u = jnp.log(1.0 + jnp.exp(power))
    return power, log_u, expo_m, jnp.exp(-0.25 * expo_m * log_u)


def pick(kind, table_ref):
    value = jnp.full(kind.shape, table_ref[0], F32)
    for index in range(1, table_ref.shape[0]):
        value = jnp.where(kind == float(index), table_ref[index], value)
    return value


def kernel(
    ngx,
    ngy,
    theta_hbm,
    terrain_hbm,
    head_hbm,
    soil_hbm,
    tiles_hbm,
    pair_ref,
    alpha_ref,
    expo_ref,
    ksat_ref,
    theta_out,
    head_out,
    th,
    sw,
    done,
    tr,
    hd,
    soil,
    soilf,
    tl,
    rows_out,
    rows_in,
    cols_out,
    cols_in,
    corner,
    gath,
    edge_out,
    edge_in,
    trs,
    trr,
    tcs,
    tcr,
    root,
    cap,
    diag,
    vec0,
    vec1,
    vec2,
    wvec,
    mom,
    momr,
    bsend,
    brecv,
    local_sem,
    out_sem,
    near_send,
    near_recv,
    g_send,
    g_recv,
    t_send,
    t_recv,
    m_send,
    m_recv,
    b_send,
    b_recv,
):
    x = lax.axis_index("gx")
    y = lax.axis_index("gy")
    levs, height, width = head_hbm.shape
    lev, th_rows, _ = theta_hbm.shape
    tile_count = width // LANES
    nblock = gath.shape[0]
    ratio = height // 2 // th_rows
    group = ngx * ngy
    me = x * ngy + y
    ext_h, ext_w = height + SUB, width + LANES
    low, high_x = x > 0, x < ngx - 1
    left, right_y = y > 0, y < ngy - 1

    loads = []

    def load(src, dst):
        copy = pltpu.make_async_copy(src, dst, local_sem.at[len(loads)])
        copy.start()
        loads.append(copy)
        return copy

    c_theta = load(theta_hbm, th)
    c_head = load(head_hbm, hd.at[:, 0:height, 0:width])
    c_soil = load(soil_hbm, soil)
    c_terrain = load(terrain_hbm, tr)
    first = x * tile_count
    total_tiles = tiles_hbm.shape[0]
    tile_at = [
        jnp.minimum(jnp.maximum(first + i - 1, 0), total_tiles - 1)
        for i in range(tile_count + 2)
    ]
    c_tiles = [load(tiles_hbm.at[tile_at[i]], tl.at[i]) for i in range(tile_count + 2)]

    rows_in[...] = jnp.zeros(rows_in.shape, F32)
    cols_in[...] = jnp.zeros(cols_in.shape, F32)
    corner[...] = jnp.zeros(corner.shape, F32)
    edge_in[...] = jnp.zeros(edge_in.shape, F32)
    trr[...] = jnp.zeros(trr.shape, F32)
    tcr[...] = jnp.zeros(tcr.shape, F32)

    barrier = pltpu.get_barrier_semaphore()

    def greet(index):
        @pl.when(index != me)
        def _():
            pl.semaphore_signal(
                barrier,
                inc=1,
                device_id={"gx": index // ngy, "gy": index % ngy},
                device_id_type=MESH,
            )

    each(group, greet)

    lane = lax.broadcasted_iota(jnp.int32, (1, LANES), 1)

    def edge_columns(source):
        first_col = jnp.zeros((th_rows, LANES), F32)
        last_col = jnp.zeros((th_rows, LANES), F32)
        for k in range(lev):
            first_col = jnp.where(lane == k, turn(source[k], k, 1), first_col)
            last_col = jnp.where(lane == k, turn(source[k], k + 1, 1), last_col)
        return first_col, last_col

    pairs = levs // 2 + 1
    upper = lax.broadcasted_iota(jnp.int32, (SUB, 1), 0) < 4

    def place(chunk):
        col = (chunk % tile_count) * LANES
        return pairs + chunk // tile_count, slice(0, SUB), slice(col, col + LANES)

    c_theta.wait()
    cols_out[0, height:] = th[:, 0, :]
    cols_out[1, height:] = th[:, th_rows - 1, :]
    for side, columns in enumerate(edge_columns(th)):
        for chunk in range(th_rows // SUB):
            rows_out[(side,) + place(chunk)] = columns[chunk * SUB : (chunk + 1) * SUB]

    c_head.wait()
    c_soil.wait()
    soilf[0:height, 0:width] = soil[...].astype(F32)
    edge_l = jnp.zeros((height, LANES), F32)
    edge_r = jnp.zeros((height, LANES), F32)
    for k in range(levs + 1):
        if k < levs:
            a, b = hd[k, 0:height, 0:LANES], hd[k, 0:height, width - LANES : width]
        else:
            a, b = soilf[0:height, 0:LANES], soilf[0:height, width - LANES : width]
        edge_l = jnp.where(lane // 4 == k, turn(a, 4 * k, 1), edge_l)
        edge_r = jnp.where((LANES - 1 - lane) // 4 == k, turn(b, -4 * k, 1), edge_r)
    cols_out[0, 0:height] = edge_l
    cols_out[1, 0:height] = edge_r
    for side, row in enumerate((0, height - SUB)):
        for p in range(pairs):
            if p < levs // 2:
                even = hd[2 * p, row : row + SUB, 0:width]
                odd = hd[2 * p + 1, row : row + SUB, 0:width]
            else:
                even = odd = soilf[row : row + SUB, 0:width]
            if side == 0:
                odd = turn(odd, 4, 0)
            else:
                even = turn(even, 4, 0)
            rows_out[side, p] = jnp.where(upper, even, odd)

    pl.semaphore_wait(barrier, group - 1)

    sent = []

    def remote(src, dst, ssem, rsem, to):
        return pltpu.make_async_remote_copy(
            src_ref=src,
            dst_ref=dst,
            send_sem=ssem,
            recv_sem=rsem,
            device_id={"gx": to[0], "gy": to[1]},
            device_id_type=MESH,
        )

    def send(cond, *what):
        @pl.when(cond)
        def _():
            remote(*what).start()

        sent.append((cond, what))

    def arrive(cond, dst, rsem):
        @pl.when(cond)
        def _():
            remote(dst, dst, near_send.at[0], rsem, (x, y)).wait_recv()

    near = []

    def halo(index, cond, src, dst, to, cond_in):
        send(cond, src, dst, near_send.at[index], near_recv.at[index], to)
        near.append((cond_in, dst, near_recv.at[index]))

    both = jnp.logical_and
    halo(0, left, rows_out.at[0], rows_in.at[0], (x, y - 1), right_y)
    halo(1, right_y, rows_out.at[1], rows_in.at[1], (x, y + 1), left)
    halo(2, low, cols_out.at[0], cols_in.at[0], (x - 1, y), high_x)
    halo(3, high_x, cols_out.at[1], cols_in.at[1], (x + 1, y), low)

    dest = x // ratio
    part = x % ratio
    offset = pl.multiple_of(part * th_rows, th_rows)
    body = ratio * th_rows

    slot = y * ratio + part
    src, dst = th.at[0], gath.at[y, pl.ds(offset, th_rows)]

    def spread(act):
        def one(i):
            @pl.when(jnp.logical_not(both(i == x, dest == y)))
            def _():
                act(remote(src, dst, g_send.at[i], g_recv.at[slot], (i, dest)))

        each(ngx, one)

    spread(lambda copy: copy.start())

    @pl.when(dest == y)
    def _():
        dst[...] = src[...]

    halo(4, both(low, left), cols_out.at[0, 0:SUB], corner.at[0], (x - 1, y - 1), both(high_x, right_y))
    halo(5, both(low, right_y), cols_out.at[0, height - SUB : height], corner.at[1], (x - 1, y + 1), both(high_x, left))
    halo(6, both(high_x, left), cols_out.at[1, 0:SUB], corner.at[2], (x + 1, y - 1), both(low, right_y))
    halo(7, both(high_x, right_y), cols_out.at[1, height - SUB : height], corner.at[3], (x + 1, y + 1), both(low, left))

    theta_in = []

    def theta_halo():
        plan = (
            (low, trs, trr, 0, (x - 1, y), high_x),
            (high_x, trs, trr, 1, (x + 1, y), low),
            (left, tcs, tcr, 0, (x, y - 1), right_y),
            (right_y, tcs, tcr, 1, (x, y + 1), left),
        )
        for index, (cond, src, dst, side, to, cond_in) in enumerate(plan):
            send(cond, src.at[side], dst.at[side], t_send.at[index], t_recv.at[index], to)
            theta_in.append((cond_in, dst.at[side], t_recv.at[index]))

    def state(k, rows, cols, alpha, expo, kmax, mask):
        power, log_u, expo_m, quarter = retention(hd[k, rows, cols], alpha, expo)
        sat = (quarter * quarter) * (quarter * quarter)
        cap[k, rows, cols] = (storage + sat) * (1.0 / time_step)
        value = jnp.sqrt(kmax) * quarter * (1.0 - jnp.exp(expo_m * (power - log_u)))
        root[k, rows, cols] = value if mask is None else jnp.where(mask, value, 0.0)

    def state_block(rows, cols, mask):
        kind = soilf[rows, cols]
        alpha, expo, kmax = (
            pick(kind, alpha_ref),
            pick(kind, expo_ref),
            pick(kind, ksat_ref),
        )
        for k in range(levs):
            state(k, rows, cols, alpha, expo, kmax, mask)

    for row in range(0, height, 32):
        state_block(slice(row, row + 32), slice(0, width), None)

    def sweep_once(source, row_below, row_above, from_right, from_left, store):
        row_at = lax.broadcasted_iota(jnp.int32, (th_rows, LANES), 0)
        metric = diffuse * tr[...]
        for k in range(lev):
            centre = source[k]
            down = jnp.where(
                row_at == th_rows - 1, row_below(k), turn(centre, -1, 0)
            )
            up = jnp.where(row_at == 0, row_above(k), turn(centre, 1, 0))
            east = jnp.where(
                lane == LANES - 1, turn(from_right, LANES - 1 - k, 1), turn(centre, -1, 1)
            )
            west = jnp.where(lane == 0, turn(from_left, -k, 1), turn(centre, 1, 1))
            flat = down + up + east + west - 4.0 * centre
            vert = -2.0 * centre
            if k > 0:
                vert = vert + source[k - 1]
            if k < lev - 1:
                vert = vert + source[k + 1]
            store(k, centre + metric * flat + vertical_mix * vert)

    def store_first(k, value):
        sw[k] = value

    first_half = lane < LANES // 2
    for r in range(ratio):

        def one(b, r=r):
            @pl.when(jnp.logical_not(both(y * ratio + r == x, b == y)))
            def _():
                arrived = gath.at[b, r * th_rows : (r + 1) * th_rows]
                remote(
                    arrived, arrived, near_send.at[0], g_recv.at[b * ratio + r], (x, y)
                ).wait_recv()

        each(nblock, one)
    for copy in c_tiles:
        copy.wait()
    grow_to = lax.broadcasted_iota(jnp.int32, (height, body), 0)
    grow_from = lax.broadcasted_iota(jnp.int32, (height, body), 1)
    grow = jnp.where(grow_from == grow_to // 2, infiltrate, 0.0).astype(F32)

    def down(i):
        total = None
        for q in range(2):
            term = dot(gath[pair_ref[q, tile_at[i]]], tl[i, q])
            total = term if total is None else total + term
        return total

    blocks = [down(i + 1) for i in range(tile_count)]
    blocks.append(jnp.where(first_half, down(tile_count + 1), down(0)))
    infil = dot(grow, jnp.concatenate(blocks, axis=1))
    edge_out[0] = infil[0:SUB]
    edge_out[1] = infil[height - SUB : height]
    vec0[0, 0:height] = infil
    edges_here = len(near)
    halo(8, left, edge_out.at[0], edge_in.at[0], (x, y - 1), right_y)
    halo(9, right_y, edge_out.at[1], edge_in.at[1], (x, y + 1), left)

    def rows_beside(k):
        below, above = rows_in[0, k // 2], rows_in[1, k // 2]
        if k % 2 == 0:
            above = turn(above, 4, 0)
        else:
            below = turn(below, 4, 0)
        return jnp.where(upper, below, above)

    for cond, dst, sem in near[:edges_here]:
        arrive(cond, dst, sem)
    for k in range(levs):
        hd[k, height:ext_h, 0:width] = rows_beside(k)
    soilf[height:ext_h, 0:width] = rows_beside(levs)
    right_side, left_side = cols_in[0, 0:height], cols_in[1, 0:height]
    right_corner = jnp.where(upper, corner[0], corner[1])
    left_corner = jnp.where(upper, corner[2], corner[3])
    for k in range(levs + 1):
        side = jnp.where(first_half, turn(right_side, -4 * k, 1), turn(left_side, 4 * k, 1))
        tip = jnp.where(first_half, turn(right_corner, -4 * k, 1), turn(left_corner, 4 * k, 1))
        if k < levs:
            hd[k, 0:height, width:ext_w] = side
            hd[k, height:ext_h, width:ext_w] = tip
        else:
            soilf[0:height, width:ext_w] = side
            soilf[height:ext_h, width:ext_w] = tip

    col_ok = jnp.logical_or(
        jnp.logical_and(lane < 4, high_x), jnp.logical_and(lane >= LANES - 4, low)
    )
    row_ok = jnp.logical_or(
        jnp.logical_and(upper, right_y), jnp.logical_and(jnp.logical_not(upper), left)
    )
    state_block(
        slice(0, height), slice(width, ext_w), jnp.broadcast_to(col_ok, (height, LANES))
    )
    state_block(
        slice(height, ext_h), slice(0, width), jnp.broadcast_to(row_ok, (SUB, width))
    )
    state_block(
        slice(height, ext_h), slice(width, ext_w), jnp.logical_and(row_ok, col_ok)
    )

    def across(value):
        return (turn(value, 1, 1) + turn(value, -1, 1)) + (
            turn(value, 1, 0) + turn(value, -1, 0)
        )

    def around(ref, k):
        total = across(ref[k])
        if k > 0:
            total = total + ref[k - 1]
        if k < levs - 1:
            total = total + ref[k + 1]
        return total

    for k in range(levs):
        wvec[0, k] = root[k] * hd[k]
    for k in reversed(range(levs)):
        centre = root[k]
        span = around(root, k)
        flow = around(wvec.at[0], k) - span * hd[k]
        if k > 0:
            flow = flow - root[k - 1]
        if k < levs - 1:
            flow = flow + root[k + 1]
        rhs = centre * flow
        if k == 0:
            for cond, dst, sem in near[edges_here:]:
                arrive(cond, dst, sem)
            edge = jnp.where(upper, edge_in[0], edge_in[1])
            rhs = rhs + jnp.concatenate([vec0[0, 0:height], edge], axis=0)
        diag[k] = cap[k] + centre * span
        vec0[k] = rhs
        wvec[1, k] = centre * rhs

    def fold(value):
        part = None
        for c in range(0, width, LANES):
            for r in range(0, height, SUB):
                piece = value[r : r + SUB, c : c + LANES]
                part = piece if part is None else part + piece
        return part

    def plus(total, value):
        return value if total is None else total + value

    sums = [None] * 6
    for k in range(levs):
        here = vec0[k]
        image = diag[k] * here - root[k] * around(wvec.at[1], k)
        vec1[k] = image
        wvec[0, k] = root[k] * image
        sums[0] = plus(sums[0], fold(here * here))
        sums[1] = plus(sums[1], fold(here * image))
        sums[2] = plus(sums[2], fold(image * image))
    for k in range(levs):
        here = vec1[k]
        image = diag[k] * here - root[k] * around(wvec.at[0], k)
        vec2[k] = image
        wvec[1, k] = root[k] * image
        sums[3] = plus(sums[3], fold(here * image))
        sums[4] = plus(sums[4], fold(image * image))
    for k in range(levs):
        here = vec2[k]
        image = diag[k] * here - root[k] * around(wvec.at[1], k)
        sums[5] = plus(sums[5], fold(here * image))

    row8 = lax.broadcasted_iota(jnp.int32, (SUB, LANES), 0)
    packed = jnp.zeros((SUB, LANES), F32)
    for index, value in enumerate(sums):
        packed = jnp.where(row8 == index, jnp.sum(value, axis=0, keepdims=True), packed)
    mom[...] = packed
    momr[me] = packed

    def tell(index):
        @pl.when(index != me)
        def _():
            remote(
                mom, momr.at[me], m_send.at[index], m_recv.at[me], (index // ngy, index % ngy)
            ).start()

    each(group, tell)

    near_count = len(sent)
    for cond, what in sent[:near_count]:

        @pl.when(cond)
        def _():
            remote(*what).wait_send()

    spread(lambda copy: copy.wait_send())
    def store_first(k, value):
        sw[k] = value

    def edge_column(side):
        pieces = [rows_in[(side,) + place(chunk)] for chunk in range(th_rows // SUB)]
        return jnp.concatenate(pieces, axis=0)

    c_terrain.wait()
    sweep_once(
        th,
        lambda k: cols_in[0, height + k : height + k + 1],
        lambda k: cols_in[1, height + k : height + k + 1],
        edge_column(0),
        edge_column(1),
        store_first,
    )
    trs[0] = sw[:, 0, :]
    trs[1] = sw[:, th_rows - 1, :]
    tcs[0], tcs[1] = edge_columns(sw)
    theta_halo()

    def hear(index):
        @pl.when(index != me)
        def _():
            remote(mom, momr.at[index], near_send.at[0], m_recv.at[index], (x, y)).wait_recv()

    each(group, hear)
    moments = jnp.sum(jnp.sum(momr[...], axis=0), axis=1, keepdims=True)
    mu = [moments[i : i + 1, :] for i in range(6)]
    scale = mu[1] / mu[0]
    inverse = mu[0] / mu[1]
    nu = []
    factor = 1.0 / mu[0]
    for i in range(6):
        nu.append(mu[i] * factor)
        factor = factor * inverse
    tiny = 1e-7
    l1, l2 = nu[2] / nu[1], nu[3] / nu[1]
    a11 = jnp.maximum(nu[3] - l1 * nu[2], tiny * nu[3])
    a12 = nu[4] - l1 * nu[3]
    b1 = nu[1] - l1 * nu[0]
    ratio_l = a12 / a11
    a22 = jnp.maximum(nu[5] - l2 * nu[3] - ratio_l * a12, tiny * nu[5])
    b2 = nu[2] - l2 * nu[0] - ratio_l * b1
    c2 = b2 / a22
    c1 = (b1 - a12 * c2) / a11
    c0 = (nu[0] - nu[2] * c1 - nu[3] * c2) / nu[1]
    c0 = c0 * inverse
    c1 = c1 * inverse * inverse
    c2 = c2 * inverse * inverse * inverse

    def advance_head(k):
        own = (k, slice(0, height), slice(0, width))
        value = hd[own] + (c0 * vec0[own] + c1 * vec1[own] + c2 * vec2[own])
        hd[own] = value
        return value

    surface = advance_head(0)
    kind = soilf[0:height, 0:width]
    _, _, _, quarter = retention(surface, pick(kind, alpha_ref), pick(kind, expo_ref))
    moist = (quarter * quarter) * (quarter * quarter)
    pair_row = lax.broadcasted_iota(jnp.int32, (body, height), 0)
    pair_col = lax.broadcasted_iota(jnp.int32, (body, height), 1)
    halver = jnp.where(pair_col // 2 == pair_row, 0.5, 0.0).astype(F32)
    halves = dot(halver, moist)
    contrib = []
    for i in range(tile_count):
        for q in range(2):
            contrib.append(
                (
                    pair_ref[q, first + i],
                    dot_nt(halves[:, i * LANES : (i + 1) * LANES], tl[i + 1, q]),
                )
            )

    for t in range(nblock):
        total = jnp.zeros((body, LANES), F32)
        for where_to, value in contrib:
            total = total + jnp.where(where_to == t, value, 0.0)
        for r in range(ratio):
            piece = total[r * th_rows : (r + 1) * th_rows]
            bsend[t * ratio + r] = piece
            to_x = y * ratio + r
            mine = jnp.logical_and(to_x == x, y == t)

            @pl.when(mine)
            def _():
                brecv[x] = piece

            @pl.when(jnp.logical_not(mine))
            def _():
                remote(
                    bsend.at[t * ratio + r],
                    brecv.at[x],
                    b_send.at[t * ratio + r],
                    b_recv.at[x],
                    (to_x, t),
                ).start()

    for k in range(1, levs):
        advance_head(k)

    out_head = pltpu.make_async_copy(hd.at[:, 0:height, 0:width], head_out, out_sem.at[1])
    out_head.start()

    def told(index):
        @pl.when(index != me)
        def _():
            remote(
                mom, momr.at[me], m_send.at[index], m_recv.at[me], (index // ngy, index % ngy)
            ).wait_send()

    each(group, told)

    for cond, dst, sem in theta_in:
        arrive(cond, dst, sem)

    def store_second(k, value):
        done[k] = value

    sweep_once(
        sw,
        lambda k: trr[0, k : k + 1],
        lambda k: trr[1, k : k + 1],
        tcr[0],
        tcr[1],
        store_second,
    )
    out_theta = pltpu.make_async_copy(done.at[1:lev], theta_out.at[1:lev], out_sem.at[0])
    out_theta.start()

    for cond, what in sent[near_count:]:

        @pl.when(cond)
        def _():
            remote(*what).wait_send()

    own_y = x // ratio

    def collect(index):
        mine = jnp.logical_and(index == x, own_y == y)

        @pl.when(jnp.logical_not(mine))
        def _():
            remote(
                brecv.at[index], brecv.at[index], near_send.at[0], b_recv.at[index], (x, y)
            ).wait_recv()

    each(ngx, collect)
    done[0] = done[0] + evaporate * jnp.sum(brecv[...], axis=0)

    out_level = pltpu.make_async_copy(done.at[0], theta_out.at[0], out_sem.at[2])
    out_level.start()
    for t in range(nblock):
        for r in range(ratio):
            to_x = y * ratio + r

            @pl.when(jnp.logical_not(jnp.logical_and(to_x == x, y == t)))
            def _():
                remote(
                    bsend.at[t * ratio + r],
                    brecv.at[x],
                    b_send.at[t * ratio + r],
                    b_recv.at[x],
                    (to_x, t),
                ).wait_send()

    out_theta.wait()
    out_head.wait()
    out_level.wait()


def shards(ngx, ngy, theta, terrain, head, soil, pair_map, tiles, vg_alpha, vg_n, ksat):
    lev, th_rows, _ = theta.shape
    levs, height, width = head.shape
    body = height // 2
    ratio = body // th_rows
    tile_count = width // LANES
    slabs = levs // 2 + 1 + pl.cdiv(th_rows // SUB, tile_count)
    ext = (levs, height + SUB, width + LANES)
    dma = pltpu.SemaphoreType.DMA
    group = ngx * ngy
    anywhere = pl.BlockSpec(memory_space=pltpu.HBM)
    scalars = pl.BlockSpec(memory_space=pltpu.SMEM)
    vmem = lambda *shape: pltpu.VMEM(shape, F32)
    return pl.pallas_call(
        functools.partial(kernel, ngx, ngy),
        out_shape=(
            jax.ShapeDtypeStruct(theta.shape, F32),
            jax.ShapeDtypeStruct(head.shape, F32),
        ),
        in_specs=[anywhere] * 5 + [scalars] * 4,
        out_specs=(anywhere, anywhere),
        scratch_shapes=[
            vmem(*theta.shape),
            vmem(*theta.shape),
            vmem(*theta.shape),
            vmem(*terrain.shape),
            vmem(*ext),
            pltpu.VMEM((height, width), jnp.int32),
            vmem(*ext[1:]),
            vmem(tile_count + 2, 2, LANES, LANES),
            vmem(2, slabs, SUB, width),
            vmem(2, slabs, SUB, width),
            vmem(2, height + lev, LANES),
            vmem(2, height + lev, LANES),
            vmem(4, SUB, LANES),
            vmem(ngy, body, LANES),
            vmem(2, SUB, width + LANES),
            vmem(2, SUB, width + LANES),
            vmem(2, lev, LANES),
            vmem(2, lev, LANES),
            vmem(2, th_rows, LANES),
            vmem(2, th_rows, LANES),
            vmem(*ext),
            vmem(*ext),
            vmem(*ext),
            vmem(*ext),
            vmem(*ext),
            vmem(*ext),
            vmem(2, *ext),
            vmem(SUB, LANES),
            vmem(group, SUB, LANES),
            vmem(ngy * ratio, th_rows, LANES),
            vmem(ngx, th_rows, LANES),
            dma((tile_count + 6,)),
            dma((3,)),
            dma((10,)),
            dma((10,)),
            dma((ngx,)),
            dma((ngy * ratio,)),
            dma((4,)),
            dma((4,)),
            dma((group,)),
            dma((group,)),
            dma((ngy * ratio,)),
            dma((ngx,)),
        ],
        compiler_params=pltpu.CompilerParams(
            collective_id=0, has_side_effects=True, vmem_limit_bytes=63 * 1024 * 1024
        ),
        name="coupled_step",
    )(theta, terrain, head, soil, tiles, pair_map.T, vg_alpha, vg_n, ksat)


def solution(mesh):
    placed = (
        P("groups", "gx", "gy"),
        P(("groups", "gx"), "gy"),
        P("groups", "gy", "gx"),
        P(("groups", "gy"), "gx"),
        P(),
        P(),
        P(),
        P(),
        P(),
    )
    return jax.shard_map(
        functools.partial(shards, mesh.shape["gx"], mesh.shape["gy"]),
        mesh=mesh,
        in_specs=placed,
        out_specs=(P("groups", "gx", "gy"), P("groups", "gy", "gx")),
        check_vma=False,
    )
```

```python
import functools

import jax
import jax.numpy as jnp
from jax import lax
from jax.experimental import pallas as pl
from jax.experimental.pallas import tpu as pltpu
from jax.sharding import PartitionSpec as P

diffuse = 0.08
vertical_mix = 0.1
time_step = 4.0
infiltrate = 0.5
evaporate = 1.0
storage = 0.1

LANES = 128
SUB = 8
MESH = pl.DeviceIdType.MESH
HIGH = lax.Precision.HIGHEST
F32 = jnp.float32


def dot(a, b):
    return jnp.dot(a, b, precision=HIGH, preferred_element_type=F32)


def dot_nt(a, b):
    return lax.dot_general(
        a, b, (((1,), (1,)), ((), ())), precision=HIGH, preferred_element_type=F32
    )


def each(count, body):
    if count <= 16:
        for index in range(count):
            body(index)
    else:

        @pl.loop(0, count)
        def _(index):
            body(index)


def turn(value, amount, axis):
    size = value.shape[axis]
    amount = amount % size
    return value if amount == 0 else pltpu.roll(value, amount, axis)


def retention(head, alpha, expo):
    expo_m = 1.0 - 1.0 / expo
    power = expo * jnp.log(alpha * jnp.abs(head))
    log_u = jnp.log(1.0 + jnp.exp(power))
    return power, log_u, expo_m, jnp.exp(-0.25 * expo_m * log_u)


def pick(kind, table_ref):
    value = jnp.full(kind.shape, table_ref[0], F32)
    for index in range(1, table_ref.shape[0]):
        value = jnp.where(kind == float(index), table_ref[index], value)
    return value


def kernel(
    ngx,
    ngy,
    theta_hbm,
    terrain_hbm,
    head_hbm,
    soil_hbm,
    tiles_hbm,
    pair_ref,
    alpha_ref,
    expo_ref,
    ksat_ref,
    theta_out,
    head_out,
    th,
    sw,
    done,
    tr,
    hd,
    soil,
    soilf,
    tl,
    rows_out,
    rows_in,
    cols_out,
    cols_in,
    corner,
    gath,
    edge_out,
    edge_in,
    trs,
    trr,
    tcs,
    tcr,
    root,
    cap,
    diag,
    vec0,
    vec1,
    vec2,
    wvec,
    mom,
    momr,
    bsend,
    brecv,
    local_sem,
    out_sem,
    near_send,
    near_recv,
    g_send,
    g_recv,
    t_send,
    t_recv,
    m_send,
    m_recv,
    b_send,
    b_recv,
):
    x = lax.axis_index("gx")
    y = lax.axis_index("gy")
    levs, height, width = head_hbm.shape
    lev, th_rows, _ = theta_hbm.shape
    tile_count = width // LANES
    nblock = gath.shape[0]
    ratio = height // 2 // th_rows
    group = ngx * ngy
    me = x * ngy + y
    ext_h, ext_w = height + SUB, width + LANES
    low, high_x = x > 0, x < ngx - 1
    left, right_y = y > 0, y < ngy - 1

    loads = []

    def load(src, dst):
        copy = pltpu.make_async_copy(src, dst, local_sem.at[len(loads)])
        copy.start()
        loads.append(copy)
        return copy

    c_theta = load(theta_hbm, th)
    c_head = load(head_hbm, hd.at[:, 0:height, 0:width])
    c_soil = load(soil_hbm, soil)
    c_terrain = load(terrain_hbm, tr)
    first = x * tile_count
    total_tiles = tiles_hbm.shape[0]
    tile_at = [
        jnp.minimum(jnp.maximum(first + i - 1, 0), total_tiles - 1)
        for i in range(tile_count + 2)
    ]
    c_tiles = [load(tiles_hbm.at[tile_at[i]], tl.at[i]) for i in range(tile_count + 2)]

    rows_in[...] = jnp.zeros(rows_in.shape, F32)
    cols_in[...] = jnp.zeros(cols_in.shape, F32)
    corner[...] = jnp.zeros(corner.shape, F32)
    edge_in[...] = jnp.zeros(edge_in.shape, F32)
    trr[...] = jnp.zeros(trr.shape, F32)
    tcr[...] = jnp.zeros(tcr.shape, F32)

    barrier = pltpu.get_barrier_semaphore()

    def greet(index):
        @pl.when(index != me)
        def _():
            pl.semaphore_signal(
                barrier,
                inc=1,
                device_id={"gx": index // ngy, "gy": index % ngy},
                device_id_type=MESH,
            )

    each(group, greet)

    lane = lax.broadcasted_iota(jnp.int32, (1, LANES), 1)

    def edge_columns(source):
        first_col = jnp.zeros((th_rows, LANES), F32)
        last_col = jnp.zeros((th_rows, LANES), F32)
        for k in range(lev):
            first_col = jnp.where(lane == k, turn(source[k], k, 1), first_col)
            last_col = jnp.where(lane == k, turn(source[k], k + 1, 1), last_col)
        return first_col, last_col

    pairs = levs // 2 + 1
    upper = lax.broadcasted_iota(jnp.int32, (SUB, 1), 0) < 4

    def place(chunk):
        col = (chunk % tile_count) * LANES
        return pairs + chunk // tile_count, slice(0, SUB), slice(col, col + LANES)

    c_theta.wait()
    cols_out[0, height:] = th[:, 0, :]
    cols_out[1, height:] = th[:, th_rows - 1, :]
    for side, columns in enumerate(edge_columns(th)):
        for chunk in range(th_rows // SUB):
            rows_out[(side,) + place(chunk)] = columns[chunk * SUB : (chunk + 1) * SUB]

    c_head.wait()
    c_soil.wait()
    soilf[0:height, 0:width] = soil[...].astype(F32)
    edge_l = jnp.zeros((height, LANES), F32)
    edge_r = jnp.zeros((height, LANES), F32)
    for k in range(levs + 1):
        if k < levs:
            a, b = hd[k, 0:height, 0:LANES], hd[k, 0:height, width - LANES : width]
        else:
            a, b = soilf[0:height, 0:LANES], soilf[0:height, width - LANES : width]
        edge_l = jnp.where(lane // 4 == k, turn(a, 4 * k, 1), edge_l)
        edge_r = jnp.where((LANES - 1 - lane) // 4 == k, turn(b, -4 * k, 1), edge_r)
    cols_out[0, 0:height] = edge_l
    cols_out[1, 0:height] = edge_r
    for side, row in enumerate((0, height - SUB)):
        for p in range(pairs):
            if p < levs // 2:
                even = hd[2 * p, row : row + SUB, 0:width]
                odd = hd[2 * p + 1, row : row + SUB, 0:width]
            else:
                even = odd = soilf[row : row + SUB, 0:width]
            if side == 0:
                odd = turn(odd, 4, 0)
            else:
                even = turn(even, 4, 0)
            rows_out[side, p] = jnp.where(upper, even, odd)

    pl.semaphore_wait(barrier, group - 1)

    sent = []

    def remote(src, dst, ssem, rsem, to):
        return pltpu.make_async_remote_copy(
            src_ref=src,
            dst_ref=dst,
            send_sem=ssem,
            recv_sem=rsem,
            device_id={"gx": to[0], "gy": to[1]},
            device_id_type=MESH,
        )

    def send(cond, *what):
        @pl.when(cond)
        def _():
            remote(*what).start()

        sent.append((cond, what))

    def arrive(cond, dst, rsem):
        @pl.when(cond)
        def _():
            remote(dst, dst, near_send.at[0], rsem, (x, y)).wait_recv()

    near = []

    def halo(index, cond, src, dst, to, cond_in):
        send(cond, src, dst, near_send.at[index], near_recv.at[index], to)
        near.append((cond_in, dst, near_recv.at[index]))

    both = jnp.logical_and
    halo(0, left, rows_out.at[0], rows_in.at[0], (x, y - 1), right_y)
    halo(1, right_y, rows_out.at[1], rows_in.at[1], (x, y + 1), left)
    halo(2, low, cols_out.at[0], cols_in.at[0], (x - 1, y), high_x)
    halo(3, high_x, cols_out.at[1], cols_in.at[1], (x + 1, y), low)

    dest = x // ratio
    part = x % ratio
    offset = pl.multiple_of(part * th_rows, th_rows)
    body = ratio * th_rows

    slot = y * ratio + part
    src, dst = th.at[0], gath.at[y, pl.ds(offset, th_rows)]

    def spread(act):
        def one(i):
            @pl.when(jnp.logical_not(both(i == x, dest == y)))
            def _():
                act(remote(src, dst, g_send.at[i], g_recv.at[slot], (i, dest)))

        each(ngx, one)

    spread(lambda copy: copy.start())

    @pl.when(dest == y)
    def _():
        dst[...] = src[...]

    halo(4, both(low, left), cols_out.at[0, 0:SUB], corner.at[0], (x - 1, y - 1), both(high_x, right_y))
    halo(5, both(low, right_y), cols_out.at[0, height - SUB : height], corner.at[1], (x - 1, y + 1), both(high_x, left))
    halo(6, both(high_x, left), cols_out.at[1, 0:SUB], corner.at[2], (x + 1, y - 1), both(low, right_y))
    halo(7, both(high_x, right_y), cols_out.at[1, height - SUB : height], corner.at[3], (x + 1, y + 1), both(low, left))

    theta_in = []

    def theta_halo():
        plan = (
            (low, trs, trr, 0, (x - 1, y), high_x),
            (high_x, trs, trr, 1, (x + 1, y), low),
            (left, tcs, tcr, 0, (x, y - 1), right_y),
            (right_y, tcs, tcr, 1, (x, y + 1), left),
        )
        for index, (cond, src, dst, side, to, cond_in) in enumerate(plan):
            send(cond, src.at[side], dst.at[side], t_send.at[index], t_recv.at[index], to)
            theta_in.append((cond_in, dst.at[side], t_recv.at[index]))

    def state(k, rows, cols, alpha, expo, kmax, mask):
        power, log_u, expo_m, quarter = retention(hd[k, rows, cols], alpha, expo)
        sat = (quarter * quarter) * (quarter * quarter)
        cap[k, rows, cols] = (storage + sat) * (1.0 / time_step)
        value = jnp.sqrt(kmax) * quarter * (1.0 - jnp.exp(expo_m * (power - log_u)))
        root[k, rows, cols] = value if mask is None else jnp.where(mask, value, 0.0)

    def state_block(rows, cols, mask):
        kind = soilf[rows, cols]
        alpha, expo, kmax = (
            pick(kind, alpha_ref),
            pick(kind, expo_ref),
            pick(kind, ksat_ref),
        )
        for k in range(levs):
            state(k, rows, cols, alpha, expo, kmax, mask)

    for row in range(0, height, 32):
        state_block(slice(row, row + 32), slice(0, width), None)

    def sweep_once(source, row_below, row_above, from_right, from_left, store):
        row_at = lax.broadcasted_iota(jnp.int32, (th_rows, LANES), 0)
        metric = diffuse * tr[...]
        for k in range(lev):
            centre = source[k]
            down = jnp.where(
                row_at == th_rows - 1, row_below(k), turn(centre, -1, 0)
            )
            up = jnp.where(row_at == 0, row_above(k), turn(centre, 1, 0))
            east = jnp.where(
                lane == LANES - 1, turn(from_right, LANES - 1 - k, 1), turn(centre, -1, 1)
            )
            west = jnp.where(lane == 0, turn(from_left, -k, 1), turn(centre, 1, 1))
            flat = down + up + east + west - 4.0 * centre
            vert = -2.0 * centre
            if k > 0:
                vert = vert + source[k - 1]
            if k < lev - 1:
                vert = vert + source[k + 1]
            store(k, centre + metric * flat + vertical_mix * vert)

    def store_first(k, value):
        sw[k] = value

    first_half = lane < LANES // 2
    for r in range(ratio):

        def one(b, r=r):
            @pl.when(jnp.logical_not(both(y * ratio + r == x, b == y)))
            def _():
                arrived = gath.at[b, r * th_rows : (r + 1) * th_rows]
                remote(
                    arrived, arrived, near_send.at[0], g_recv.at[b * ratio + r], (x, y)
                ).wait_recv()

        each(nblock, one)
    for copy in c_tiles:
        copy.wait()
    grow_to = lax.broadcasted_iota(jnp.int32, (height, body), 0)
    grow_from = lax.broadcasted_iota(jnp.int32, (height, body), 1)
    grow = jnp.where(grow_from == grow_to // 2, infiltrate, 0.0).astype(F32)

    def down(i):
        total = None
        for q in range(2):
            term = dot(gath[pair_ref[q, tile_at[i]]], tl[i, q])
            total = term if total is None else total + term
        return total

    blocks = [down(i + 1) for i in range(tile_count)]
    blocks.append(jnp.where(first_half, down(tile_count + 1), down(0)))
    infil = dot(grow, jnp.concatenate(blocks, axis=1))
    edge_out[0] = infil[0:SUB]
    edge_out[1] = infil[height - SUB : height]
    vec0[0, 0:height] = infil
    edges_here = len(near)
    halo(8, left, edge_out.at[0], edge_in.at[0], (x, y - 1), right_y)
    halo(9, right_y, edge_out.at[1], edge_in.at[1], (x, y + 1), left)

    def rows_beside(k):
        below, above = rows_in[0, k // 2], rows_in[1, k // 2]
        if k % 2 == 0:
            above = turn(above, 4, 0)
        else:
            below = turn(below, 4, 0)
        return jnp.where(upper, below, above)

    for cond, dst, sem in near[:edges_here]:
        arrive(cond, dst, sem)
    for k in range(levs):
        hd[k, height:ext_h, 0:width] = rows_beside(k)
    soilf[height:ext_h, 0:width] = rows_beside(levs)
    right_side, left_side = cols_in[0, 0:height], cols_in[1, 0:height]
    right_corner = jnp.where(upper, corner[0], corner[1])
    left_corner = jnp.where(upper, corner[2], corner[3])
    for k in range(levs + 1):
        side = jnp.where(first_half, turn(right_side, -4 * k, 1), turn(left_side, 4 * k, 1))
        tip = jnp.where(first_half, turn(right_corner, -4 * k, 1), turn(left_corner, 4 * k, 1))
        if k < levs:
            hd[k, 0:height, width:ext_w] = side
            hd[k, height:ext_h, width:ext_w] = tip
        else:
            soilf[0:height, width:ext_w] = side
            soilf[height:ext_h, width:ext_w] = tip

    col_ok = jnp.logical_or(
        jnp.logical_and(lane < 4, high_x), jnp.logical_and(lane >= LANES - 4, low)
    )
    row_ok = jnp.logical_or(
        jnp.logical_and(upper, right_y), jnp.logical_and(jnp.logical_not(upper), left)
    )
    state_block(
        slice(0, height), slice(width, ext_w), jnp.broadcast_to(col_ok, (height, LANES))
    )
    state_block(
        slice(height, ext_h), slice(0, width), jnp.broadcast_to(row_ok, (SUB, width))
    )
    state_block(
        slice(height, ext_h), slice(width, ext_w), jnp.logical_and(row_ok, col_ok)
    )

    def across(value):
        return (turn(value, 1, 1) + turn(value, -1, 1)) + (
            turn(value, 1, 0) + turn(value, -1, 0)
        )

    def around(ref, k):
        total = across(ref[k])
        if k > 0:
            total = total + ref[k - 1]
        if k < levs - 1:
            total = total + ref[k + 1]
        return total

    for k in range(levs):
        wvec[0, k] = root[k] * hd[k]
    for k in reversed(range(levs)):
        centre = root[k]
        span = around(root, k)
        flow = around(wvec.at[0], k) - span * hd[k]
        if k > 0:
            flow = flow - root[k - 1]
        if k < levs - 1:
            flow = flow + root[k + 1]
        rhs = centre * flow
        if k == 0:
            for cond, dst, sem in near[edges_here:]:
                arrive(cond, dst, sem)
            edge = jnp.where(upper, edge_in[0], edge_in[1])
            rhs = rhs + jnp.concatenate([vec0[0, 0:height], edge], axis=0)
        diag[k] = cap[k] + centre * span
        vec0[k] = rhs
        wvec[1, k] = centre * rhs

    def fold(value):
        part = None
        for c in range(0, width, LANES):
            for r in range(0, height, SUB):
                piece = value[r : r + SUB, c : c + LANES]
                part = piece if part is None else part + piece
        return part

    def plus(total, value):
        return value if total is None else total + value

    sums = [None] * 6
    for k in range(levs):
        here = vec0[k]
        image = diag[k] * here - root[k] * around(wvec.at[1], k)
        vec1[k] = image
        wvec[0, k] = root[k] * image
        sums[0] = plus(sums[0], fold(here * here))
        sums[1] = plus(sums[1], fold(here * image))
        sums[2] = plus(sums[2], fold(image * image))
    for k in range(levs):
        here = vec1[k]
        image = diag[k] * here - root[k] * around(wvec.at[0], k)
        vec2[k] = image
        wvec[1, k] = root[k] * image
        sums[3] = plus(sums[3], fold(here * image))
        sums[4] = plus(sums[4], fold(image * image))
    for k in range(levs):
        here = vec2[k]
        image = diag[k] * here - root[k] * around(wvec.at[1], k)
        sums[5] = plus(sums[5], fold(here * image))

    row8 = lax.broadcasted_iota(jnp.int32, (SUB, LANES), 0)
    packed = jnp.zeros((SUB, LANES), F32)
    for index, value in enumerate(sums):
        packed = jnp.where(row8 == index, jnp.sum(value, axis=0, keepdims=True), packed)
    def line(stage, count, at, to, act):
        def one(index):
            @pl.when(index != at)
            def _():
                act(
                    remote(
                        mom.at[stage],
                        momr.at[stage, at],
                        m_send.at[stage, index],
                        m_recv.at[stage, at],
                        to(index),
                    )
                )

        each(count, one)

    def hear(stage, count, at):
        def one(index):
            @pl.when(index != at)
            def _():
                arrived = momr.at[stage, index]
                remote(
                    arrived, arrived, near_send.at[0], m_recv.at[stage, index], (x, y)
                ).wait_recv()

        each(count, one)
        return jnp.sum(momr[stage, 0:count], axis=0)

    along_y = (0, ngy, y, lambda index: (x, index))
    along_x = (1, ngx, x, lambda index: (index, y))
    mom[0] = packed
    momr[0, y] = packed
    line(*along_y, lambda copy: copy.start())

    near_count = len(sent)
    for cond, what in sent[:near_count]:

        @pl.when(cond)
        def _():
            remote(*what).wait_send()

    spread(lambda copy: copy.wait_send())
    def store_first(k, value):
        sw[k] = value

    def edge_column(side):
        pieces = [rows_in[(side,) + place(chunk)] for chunk in range(th_rows // SUB)]
        return jnp.concatenate(pieces, axis=0)

    c_terrain.wait()
    sweep_once(
        th,
        lambda k: cols_in[0, height + k : height + k + 1],
        lambda k: cols_in[1, height + k : height + k + 1],
        edge_column(0),
        edge_column(1),
        store_first,
    )
    trs[0] = sw[:, 0, :]
    trs[1] = sw[:, th_rows - 1, :]
    tcs[0], tcs[1] = edge_columns(sw)
    theta_halo()

    subtotal = hear(0, ngy, y)
    mom[1] = subtotal
    momr[1, x] = subtotal
    line(*along_x, lambda copy: copy.start())
    moments = jnp.sum(hear(1, ngx, x), axis=1, keepdims=True)
    mu = [moments[i : i + 1, :] for i in range(6)]
    scale = mu[1] / mu[0]
    inverse = mu[0] / mu[1]
    nu = []
    factor = 1.0 / mu[0]
    for i in range(6):
        nu.append(mu[i] * factor)
        factor = factor * inverse
    tiny = 1e-7
    l1, l2 = nu[2] / nu[1], nu[3] / nu[1]
    a11 = jnp.maximum(nu[3] - l1 * nu[2], tiny * nu[3])
    a12 = nu[4] - l1 * nu[3]
    b1 = nu[1] - l1 * nu[0]
    ratio_l = a12 / a11
    a22 = jnp.maximum(nu[5] - l2 * nu[3] - ratio_l * a12, tiny * nu[5])
    b2 = nu[2] - l2 * nu[0] - ratio_l * b1
    c2 = b2 / a22
    c1 = (b1 - a12 * c2) / a11
    c0 = (nu[0] - nu[2] * c1 - nu[3] * c2) / nu[1]
    c0 = c0 * inverse
    c1 = c1 * inverse * inverse
    c2 = c2 * inverse * inverse * inverse

    def advance_head(k):
        own = (k, slice(0, height), slice(0, width))
        value = hd[own] + (c0 * vec0[own] + c1 * vec1[own] + c2 * vec2[own])
        hd[own] = value
        return value

    surface = advance_head(0)
    kind = soilf[0:height, 0:width]
    _, _, _, quarter = retention(surface, pick(kind, alpha_ref), pick(kind, expo_ref))
    moist = (quarter * quarter) * (quarter * quarter)
    pair_row = lax.broadcasted_iota(jnp.int32, (body, height), 0)
    pair_col = lax.broadcasted_iota(jnp.int32, (body, height), 1)
    halver = jnp.where(pair_col // 2 == pair_row, 0.5, 0.0).astype(F32)
    halves = dot(halver, moist)
    contrib = []
    for i in range(tile_count):
        for q in range(2):
            contrib.append(
                (
                    pair_ref[q, first + i],
                    dot_nt(halves[:, i * LANES : (i + 1) * LANES], tl[i + 1, q]),
                )
            )

    for t in range(nblock):
        total = jnp.zeros((body, LANES), F32)
        for where_to, value in contrib:
            total = total + jnp.where(where_to == t, value, 0.0)
        for r in range(ratio):
            piece = total[r * th_rows : (r + 1) * th_rows]
            bsend[t * ratio + r] = piece
            to_x = y * ratio + r
            mine = jnp.logical_and(to_x == x, y == t)

            @pl.when(mine)
            def _():
                brecv[x] = piece

            @pl.when(jnp.logical_not(mine))
            def _():
                remote(
                    bsend.at[t * ratio + r],
                    brecv.at[x],
                    b_send.at[t * ratio + r],
                    b_recv.at[x],
                    (to_x, t),
                ).start()

    for k in range(1, levs):
        advance_head(k)

    out_head = pltpu.make_async_copy(hd.at[:, 0:height, 0:width], head_out, out_sem.at[1])
    out_head.start()

    line(*along_y, lambda copy: copy.wait_send())
    line(*along_x, lambda copy: copy.wait_send())

    for cond, dst, sem in theta_in:
        arrive(cond, dst, sem)

    def store_second(k, value):
        done[k] = value

    sweep_once(
        sw,
        lambda k: trr[0, k : k + 1],
        lambda k: trr[1, k : k + 1],
        tcr[0],
        tcr[1],
        store_second,
    )
    out_theta = pltpu.make_async_copy(done.at[1:lev], theta_out.at[1:lev], out_sem.at[0])
    out_theta.start()

    for cond, what in sent[near_count:]:

        @pl.when(cond)
        def _():
            remote(*what).wait_send()

    own_y = x // ratio

    def collect(index):
        mine = jnp.logical_and(index == x, own_y == y)

        @pl.when(jnp.logical_not(mine))
        def _():
            remote(
                brecv.at[index], brecv.at[index], near_send.at[0], b_recv.at[index], (x, y)
            ).wait_recv()

    each(ngx, collect)
    done[0] = done[0] + evaporate * jnp.sum(brecv[...], axis=0)

    out_level = pltpu.make_async_copy(done.at[0], theta_out.at[0], out_sem.at[2])
    out_level.start()
    for t in range(nblock):
        for r in range(ratio):
            to_x = y * ratio + r

            @pl.when(jnp.logical_not(jnp.logical_and(to_x == x, y == t)))
            def _():
                remote(
                    bsend.at[t * ratio + r],
                    brecv.at[x],
                    b_send.at[t * ratio + r],
                    b_recv.at[x],
                    (to_x, t),
                ).wait_send()

    out_theta.wait()
    out_head.wait()
    out_level.wait()


def shards(ngx, ngy, theta, terrain, head, soil, pair_map, tiles, vg_alpha, vg_n, ksat):
    lev, th_rows, _ = theta.shape
    levs, height, width = head.shape
    body = height // 2
    ratio = body // th_rows
    tile_count = width // LANES
    slabs = levs // 2 + 1 + pl.cdiv(th_rows // SUB, tile_count)
    ext = (levs, height + SUB, width + LANES)
    dma = pltpu.SemaphoreType.DMA
    anywhere = pl.BlockSpec(memory_space=pltpu.HBM)
    scalars = pl.BlockSpec(memory_space=pltpu.SMEM)
    vmem = lambda *shape: pltpu.VMEM(shape, F32)
    return pl.pallas_call(
        functools.partial(kernel, ngx, ngy),
        out_shape=(
            jax.ShapeDtypeStruct(theta.shape, F32),
            jax.ShapeDtypeStruct(head.shape, F32),
        ),
        in_specs=[anywhere] * 5 + [scalars] * 4,
        out_specs=(anywhere, anywhere),
        scratch_shapes=[
            vmem(*theta.shape),
            vmem(*theta.shape),
            vmem(*theta.shape),
            vmem(*terrain.shape),
            vmem(*ext),
            pltpu.VMEM((height, width), jnp.int32),
            vmem(*ext[1:]),
            vmem(tile_count + 2, 2, LANES, LANES),
            vmem(2, slabs, SUB, width),
            vmem(2, slabs, SUB, width),
            vmem(2, height + lev, LANES),
            vmem(2, height + lev, LANES),
            vmem(4, SUB, LANES),
            vmem(ngy, body, LANES),
            vmem(2, SUB, width + LANES),
            vmem(2, SUB, width + LANES),
            vmem(2, lev, LANES),
            vmem(2, lev, LANES),
            vmem(2, th_rows, LANES),
            vmem(2, th_rows, LANES),
            vmem(*ext),
            vmem(*ext),
            vmem(*ext),
            vmem(*ext),
            vmem(*ext),
            vmem(*ext),
            vmem(2, *ext),
            vmem(2, SUB, LANES),
            vmem(2, max(ngx, ngy), SUB, LANES),
            vmem(ngy * ratio, th_rows, LANES),
            vmem(ngx, th_rows, LANES),
            dma((tile_count + 6,)),
            dma((3,)),
            dma((10,)),
            dma((10,)),
            dma((ngx,)),
            dma((ngy * ratio,)),
            dma((4,)),
            dma((4,)),
            dma((2, max(ngx, ngy))),
            dma((2, max(ngx, ngy))),
            dma((ngy * ratio,)),
            dma((ngx,)),
        ],
        compiler_params=pltpu.CompilerParams(
            collective_id=0, has_side_effects=True, vmem_limit_bytes=63 * 1024 * 1024
        ),
        name="coupled_step",
    )(theta, terrain, head, soil, tiles, pair_map.T, vg_alpha, vg_n, ksat)


def solution(mesh):
    placed = (
        P("groups", "gx", "gy"),
        P(("groups", "gx"), "gy"),
        P("groups", "gy", "gx"),
        P(("groups", "gy"), "gx"),
        P(),
        P(),
        P(),
        P(),
        P(),
    )
    return jax.shard_map(
        functools.partial(shards, mesh.shape["gx"], mesh.shape["gy"]),
        mesh=mesh,
        in_specs=placed,
        out_specs=(P("groups", "gx", "gy"), P("groups", "gy", "gx")),
        check_vma=False,
    )
```
